512 devices in a mesh: gx: 64 (over x, z), gz: 8 (over y, core).
Axes of the slice: x: 4, y: 4, z: 16, core: 2. Of those that a mesh axis runs over, the one named last changes fastest.
Arguments:
- velocity: float32 [2048, 64, 1024], P('gx', None, 'gz'), may hold values from -6 to 6
- register: float32 [2048, 64, 1024], P('gx', None, 'gz'), may hold values from -6 to 6
- eddy_viscosity: bfloat16 [2048, 64, 1024], P('gx', None, 'gz'), may hold values from 0.019897461 to 0.19921875
- courant: float32 [2048], P('gx'), may hold values from 200 to 20000
- inflow: float32 [64, 1024], P(None, 'gz'), may hold values from 0.5 to 1.5
Outputs:
- new_velocity: float32 [2048, 64, 1024], P('gx', None, 'gz')
- new_register: float32 [2048, 64, 1024], P('gx', None, 'gz')
The draws below stay inside these ranges and needn't reach their ends.
All inputs are finite; a program needn't handle non-finite values.
Results may differ from the reference program's by a relative error of at most 0.0017.
The reference program's roundings to bfloat16 on the way count: a program that leaves them out, or rounds other values in their place, can miss the bound.
Values may be sent and summed in bfloat16 or wider, within the bound.
No kernel may reach another device: no remote copies, remote signals or barrier semaphores. Data moves between devices by JAX's collectives and lax.ppermute only.
A program may use at most 64 MiB of HBM per device.

```python
import math
import jax
import jax.numpy as jnp
from jax import lax

NY = 64
NZ = 1024
NX = 2048


def block_scale(own_key, dims, cuts, least, high):
    def one(axis_at, blocks):
        heights = jax.random.uniform(jax.random.fold_in(jax.random.fold_in(own_key, 6), axis_at), (blocks,), jnp.float32, least / len(cuts), high / len(cuts))
        return jnp.repeat(jnp.exp(heights), dims[axis_at] // blocks).reshape((-1,) + (1,) * (len(dims) - axis_at - 1))

    loudness = one(*cuts[0])
    for cut in cuts[1:]:
        loudness = loudness * one(*cut)
    return loudness


def noise(own_key, dims, width, bound, cuts=(), held_as=jnp.bfloat16):
    level = block_scale(own_key, dims, cuts, -0.22, 0.18) if cuts else 1.0
    values = jax.random.normal(own_key, dims, jnp.float32) * width * level
    return jnp.minimum(jnp.maximum(values, -bound), bound).astype(held_as)


def setup_inputs(seed: int = 0) -> dict:
    key_of = jax.random.split(jax.random.key(seed), 6)
    return {
        "velocity": noise(key_of[0], (NX, NY, NZ), 1.0, 6.0, ((0, 64), (2, 8)), jnp.float32),
        "register": noise(key_of[1], (NX, NY, NZ), 1.0, 6.0, ((0, 64), (2, 8)), jnp.float32),
        "eddy_viscosity": jnp.clip(jnp.exp(math.log(0.19921875) - 2.3038113 * jax.random.uniform(key_of[2], (NX, NY, NZ), jnp.float32) ** block_scale(key_of[2], (NX, NY, NZ), ((0, 64), (2, 8)), -0.2, 0.2)), 0.019897461, 0.19921875).astype(jnp.bfloat16),
        "courant": jnp.clip(jnp.exp(math.log(20000.0) - 4.6051702 * jax.random.uniform(key_of[3], (NX,), jnp.float32) ** block_scale(key_of[3], (NX,), ((0, 64),), -0.2, 0.2)), 200.0, 20000.0),
        "inflow": jnp.clip(0.5 + 1.0 * jax.random.uniform(key_of[4], (NY, NZ), jnp.float32) ** block_scale(key_of[4], (NY, NZ), ((1, 8),), -0.2, 0.2), 0.5, 1.5),
    }


coef_zero = -49.0 / 18.0
coef_one = 1.5
coef_two = -3.0 / 20.0
coef_three = 1.0 / 90.0


def stencil_x(field):
    count = field.shape[0]
    padded = jnp.pad(field, ((3, 3), (0, 0), (0, 0)))
    return (coef_zero * field + coef_one * (padded[2:count + 2] + padded[4:count + 4])
            + coef_two * (padded[1:count + 1] + padded[5:count + 5])
            + coef_three * (padded[0:count] + padded[6:count + 6]))


def stencil_y(field):
    total = coef_zero * field
    for shift_by, weight in ((1, coef_one), (2, coef_two), (3, coef_three)):
        total = total + weight * (jnp.roll(field, shift_by, axis=1) + jnp.roll(field, -shift_by, axis=1))
    return total


def span_tables(length):
    position = jnp.arange(length, dtype=jnp.int32)
    product = (position[:, None] * position[None, :]) % length
    angle = product.astype(jnp.float32) * (2.0 * math.pi / length)
    wave = jnp.minimum(position, length - position).astype(jnp.float32) * (2.0 * math.pi / length)
    factor = -(wave * wave) / length
    return jnp.cos(angle).astype(jnp.bfloat16), jnp.sin(angle).astype(jnp.bfloat16), factor


def span_second(plane, cos_table, sin_table, factor):
    cosine_part = jnp.dot(plane, cos_table, preferred_element_type=jnp.float32)
    sine_part = jnp.dot(plane, sin_table, preferred_element_type=jnp.float32)
    scaled_cos = (cosine_part * factor).astype(jnp.bfloat16)
    scaled_sin = (sine_part * factor).astype(jnp.bfloat16)
    result = jnp.dot(scaled_cos, cos_table, preferred_element_type=jnp.float32)
    result = result + jnp.dot(scaled_sin, sin_table, preferred_element_type=jnp.float32)
    return result.astype(jnp.bfloat16)


def reference(velocity, register, eddy_viscosity, courant, inflow):
    cos_table, sin_table, factor = span_tables(velocity.shape[2])
    rounded = velocity.astype(jnp.bfloat16)
    second_z = lax.map(lambda plane: span_second(plane, cos_table, sin_table, factor), rounded)
    total = stencil_x(velocity) + stencil_y(velocity) + second_z.astype(jnp.float32)
    new_register = -5.0 / 9.0 * register + eddy_viscosity.astype(jnp.float32) * total
    provisional = velocity + 15.0 / 16.0 * new_register
    keep = courant / (1.0 + courant)
    take = 1.0 / (1.0 + courant)

    def advance(previous, inputs):
        station, keep_one, take_one = inputs
        current = take_one * station + keep_one * previous
        return current, current

    _, new_velocity = lax.scan(advance, inflow.astype(jnp.float32), (provisional, keep, take))
    return new_velocity, new_register
```

```python
import math

import jax
import jax.numpy as jnp
import numpy as np
from jax import lax
from jax.experimental import pallas as pl
from jax.experimental.pallas import tpu as pltpu
from jax.sharding import PartitionSpec as P

coef_zero = -49.0 / 18.0
coef_one = 1.5
coef_two = -3.0 / 20.0
coef_three = 1.0 / 90.0
decay = -5.0 / 9.0
weight = 15.0 / 16.0

STATIONS, NY, WIDTH, PARTS = 32, 64, 128, 8
LENGTH = WIDTH * PARTS
ROWS = STATIONS * NY // PARTS
VMEM_LIMIT = 16 * 1024 * 1024
F32, BF16 = jnp.float32, jnp.bfloat16
PAYLOAD = NY + 16

GROUPS = (
    [[x * 16 + h * 4 + l for l in range(4)] for x in range(4) for h in range(4)],
    [[x * 16 + h * 4 + l for h in range(4)] for x in range(4) for l in range(4)],
    [[x * 16 + z for x in range(4)] for z in range(16)],
)


def span_tables():
    position = np.arange(LENGTH, dtype=np.int64)
    product = position[:, None] * position[None, 1 : LENGTH // 2 + 1] % LENGTH
    angle = product.astype(np.float32) * np.float32(2.0 * math.pi / LENGTH)
    table = np.concatenate([np.cos(angle), np.sin(angle)], axis=1).astype(BF16)
    wave = np.arange(1, LENGTH // 2 + 1).astype(np.float32) * np.float32(2.0 * math.pi / LENGTH)
    factor = -(wave * wave) / np.float32(LENGTH)
    twice = np.where(np.arange(1, LENGTH // 2 + 1) < LENGTH // 2, 2.0, 1.0).astype(np.float32)
    factor = np.concatenate([factor * twice] * 2)[None, :].astype(np.float32)
    return table, factor


def stencil_kernel(keep, take, velocity, register, eddy, low, high, base, offset):
    def plane(i):
        if i < 0:
            return low[i + 3].astype(F32)
        if i >= STATIONS:
            return high[i - STATIONS].astype(F32)
        return velocity[i]

    running = jnp.zeros((NY, WIDTH), F32)
    for i in range(STATIONS):
        here = velocity[i]
        total = (2.0 * coef_zero) * here
        for shift, coef in ((1, coef_one), (2, coef_two), (3, coef_three)):
            along = plane(i - shift) + plane(i + shift)
            across = pltpu.roll(here, shift, 0) + pltpu.roll(here, NY - shift, 0)
            total = total + coef * (along + across)
        part = decay * register[i] + eddy[i].astype(F32) * total
        base[i] = part
        running = keep[i] * running + take[i] * (here + weight * part)
    offset[...] = running


def span_kernel(lines, table, factor, out, scaled):
    whole = jnp.concatenate([lines[b] for b in range(PARTS)], axis=1)
    step = 256
    for n in range(LENGTH // step):
        cut = slice(n * step, (n + 1) * step)
        part = jnp.dot(whole, table[:, cut], preferred_element_type=F32)
        scaled[:, cut] = (part * factor[:, cut]).astype(BF16)
    for n in range(LENGTH // step):
        part = lax.dot_general(
            scaled[...],
            table[n * step : (n + 1) * step, :],
            (((1,), (1,)), ((), ())),
            preferred_element_type=F32,
        ).astype(BF16)
        for b in range(step // WIDTH):
            out[n * step // WIDTH + b] = part[:, b * WIDTH : (b + 1) * WIDTH]


def store_payload(out, plane, gain):
    upper = gain.astype(BF16).astype(F32)
    tail = jnp.concatenate([upper, gain - upper], axis=0).astype(BF16)
    plane = plane.astype(BF16)
    for m in range(4):
        out[m, 0:NY] = plane
        out[m, NY:PAYLOAD] = tail


def offset_kernel(keep, take, second, eddy, base_offset, out):
    running = jnp.zeros((NY, WIDTH), F32)
    gain = jnp.ones((8, WIDTH), F32)
    for i in range(STATIONS):
        term = eddy[i].astype(F32) * second[i].astype(F32)
        running = keep[i] * running + (take[i] * weight) * term
        gain = gain * keep[i]
    store_payload(out, running + base_offset[...], gain)


def local_kernel(keep, take, velocity, base, eddy, second, _, register, local):
    running = jnp.zeros((NY, WIDTH), F32)
    for i in range(STATIONS):
        new = base[i] + eddy[i].astype(F32) * second[i].astype(F32)
        register[i] = new
        running = keep[i] * running + take[i] * (velocity[i] + weight * new)
        local[i] = running


def fold(place, received):
    total = jnp.zeros((NY, WIDTH), F32)
    gain = jnp.ones((8, WIDTH), F32)
    before, gain_before = total, gain
    for m in range(4):
        reached = place == m
        before = jnp.where(reached, total, before)
        gain_before = jnp.where(reached, gain, gain_before)
        tail = received[m, NY:PAYLOAD].astype(F32)
        one = tail[0:8] + tail[8:16]
        total = total * one[0:1] + received[m, 0:NY].astype(F32)
        gain = gain * one
    return before, gain_before, total, gain


def fold_kernel(place, received, before, gain_before, out):
    one, two, total, gain = fold(place[0], received)
    before[...] = one
    gain_before[...] = two
    store_payload(out, total, gain)


def final_kernel(place, keep, received, before1, gain1, before2, gain2, inflow, local, out, entering):
    step = pl.program_id(0)
    count = out.shape[0]

    @pl.when(step == 0)
    def _():
        before, gain, _, _ = fold(place[0], received)
        value = before + gain[0:1] * inflow[...]
        value = before2[...] + gain2[0:1] * value
        entering[...] = before1[...] + gain1[0:1] * value

    running = entering[...]
    for i in range(count):
        running = running * keep[step * count + i]
        out[i] = local[i] + running
    entering[...] = running


SMEM = pl.BlockSpec(memory_space=pltpu.SMEM)
VMEM = pl.BlockSpec(memory_space=pltpu.VMEM)
ANY = pl.BlockSpec(memory_space=pl.ANY)
CUBE = jax.ShapeDtypeStruct((STATIONS, NY, WIDTH), F32)
PLANE = jax.ShapeDtypeStruct((NY, WIDTH), F32)
GAIN = jax.ShapeDtypeStruct((8, WIDTH), F32)
SLOTS = jax.ShapeDtypeStruct((4, PAYLOAD, WIDTH), BF16)


def call(kernel, name, in_specs, out_shape, flops, bytes_accessed, scratch=()):
    many = isinstance(out_shape, tuple)
    return pl.pallas_call(
        kernel,
        name=name,
        in_specs=in_specs,
        out_specs=tuple(VMEM for _ in out_shape) if many else VMEM,
        out_shape=out_shape,
        scratch_shapes=scratch,
        compiler_params=pltpu.CompilerParams(vmem_limit_bytes=VMEM_LIMIT),
        cost_estimate=pl.CostEstimate(flops=flops, bytes_accessed=bytes_accessed, transcendentals=0),
    )


def body(velocity, register, eddy_viscosity, courant, inflow):
    table, factor = span_tables()
    place = lax.axis_index("gx")
    places = [jnp.reshape(p, (1,)) for p in (place % 4, place // 4 % 4, place // 16)]
    keep = courant / (1.0 + courant)
    take = 1.0 / (1.0 + courant)

    rounded = velocity.astype(BF16)
    lines = lax.all_to_all(rounded.reshape(PARTS, ROWS, WIDTH), "gz", 0, 0, tiled=True)

    count = lax.axis_size("gx")
    forward = [(i, i + 1) for i in range(count - 1)]
    backward = [(b, a) for a, b in forward]
    low = lax.ppermute(rounded[STATIONS - 3 :], "gx", forward)
    high = lax.ppermute(rounded[:3], "gx", backward)
    base, base_offset = call(
        stencil_kernel, "stencil", [SMEM, SMEM] + [VMEM] * 5, (CUBE, PLANE), 8_000_000, 4_000_000
    )(keep, take, velocity, register, eddy_viscosity, low, high)

    derived = call(
        span_kernel,
        "span",
        [VMEM, VMEM, VMEM],
        jax.ShapeDtypeStruct((PARTS, ROWS, WIDTH), BF16),
        4 * ROWS * LENGTH * LENGTH,
        3_200_000,
        (pltpu.VMEM((ROWS, LENGTH), BF16),),
    )(lines, jnp.asarray(table), jnp.asarray(factor))
    second = lax.all_to_all(derived, "gz", 0, 0, tiled=True).reshape(STATIONS, NY, WIDTH)

    payload = call(offset_kernel, "offset", [SMEM, SMEM] + [VMEM] * 3, SLOTS, 1_500_000, 1_100_000)(
        keep, take, second, eddy_viscosity, base_offset
    )
    new_register, local = call(
        local_kernel, "local", [SMEM, SMEM] + [VMEM] * 4 + [ANY], (CUBE, CUBE), 3_000_000, 5_000_000
    )(keep, take, velocity, base, eddy_viscosity, second, payload)

    found = []
    for level in range(3):
        payload = lax.all_to_all(payload, "gx", 0, 0, axis_index_groups=GROUPS[level], tiled=True)
        if level < 2:
            before, gain, payload = call(
                fold_kernel, "fold", [SMEM, VMEM], (PLANE, GAIN, SLOTS), 200_000, 300_000
            )(places[level], payload)
            found += [before, gain]

    chunk = 8
    whole = lambda *shape: pl.BlockSpec(shape, lambda i: (0,) * len(shape))
    cube = pl.BlockSpec((chunk, NY, WIDTH), lambda i: (i, 0, 0))
    new_velocity = pl.pallas_call(
        final_kernel,
        name="final",
        grid=(STATIONS // chunk,),
        in_specs=[SMEM, SMEM, whole(4, PAYLOAD, WIDTH)]
        + [whole(NY, WIDTH), whole(8, WIDTH)] * 2
        + [whole(NY, WIDTH), cube],
        out_specs=cube,
        out_shape=CUBE,
        scratch_shapes=[pltpu.VMEM((NY, WIDTH), F32)],
        compiler_params=pltpu.CompilerParams(vmem_limit_bytes=VMEM_LIMIT),
        cost_estimate=pl.CostEstimate(flops=800_000, bytes_accessed=2_300_000, transcendentals=0),
    )(places[2], keep, payload, *found, inflow, local)
    return new_velocity, new_register


def solution(mesh):
    return jax.shard_map(
        body,
        mesh=mesh,
        in_specs=(
            P("gx", None, "gz"),
            P("gx", None, "gz"),
            P("gx", None, "gz"),
            P("gx"),
            P(None, "gz"),
        ),
        out_specs=(P("gx", None, "gz"), P("gx", None, "gz")),
        check_vma=False,
    )
```

```python
import math

import jax
import jax.numpy as jnp
import numpy as np
from jax import lax
from jax.experimental import pallas as pl
from jax.experimental.pallas import tpu as pltpu
from jax.sharding import PartitionSpec as P

coef_zero = -49.0 / 18.0
coef_one = 1.5
coef_two = -3.0 / 20.0
coef_three = 1.0 / 90.0
decay = -5.0 / 9.0
weight = 15.0 / 16.0

STATIONS, NY, WIDTH, PARTS = 32, 64, 128, 8
CUTS = 4
LENGTH = WIDTH * PARTS
ROWS = STATIONS * NY // PARTS
MIB = 1024 * 1024
LARGE = 62
F32, BF16 = jnp.float32, jnp.bfloat16
PAYLOAD = NY + 16

GROUPS = (
    [[x * 16 + h * 4 + l for l in range(4)] for x in range(4) for h in range(4)],
    [[x * 16 + h * 4 + l for h in range(4)] for x in range(4) for l in range(4)],
    [[x * 16 + z for x in range(4)] for z in range(16)],
)


def span_tables():
    position = np.arange(LENGTH, dtype=np.int64)
    product = position[:, None] * position[None, 1 : LENGTH // 2 + 1] % LENGTH
    angle = product.astype(np.float32) * np.float32(2.0 * math.pi / LENGTH)
    table = np.concatenate([np.cos(angle), np.sin(angle)], axis=1).astype(BF16)
    wave = np.arange(1, LENGTH // 2 + 1).astype(np.float32) * np.float32(2.0 * math.pi / LENGTH)
    factor = -(wave * wave) / np.float32(LENGTH)
    twice = np.where(np.arange(1, LENGTH // 2 + 1) < LENGTH // 2, 2.0, 1.0).astype(np.float32)
    factor = np.concatenate([factor * twice] * 2)[None, :].astype(np.float32)
    return table, factor


def round_kernel(velocity, rounded, first, last, wide, narrow, in_sem, out_sem):
    step = STATIONS // CUTS
    cuts = [pl.ds(c * step, step) for c in range(CUTS)]
    order = [0, CUTS - 1, *range(1, CUTS - 1)]
    loads = {c: pltpu.make_async_copy(velocity.at[cuts[c]], wide.at[cuts[c]], in_sem.at[c]) for c in order}
    stores = {c: pltpu.make_async_copy(narrow.at[cuts[c]], rounded.at[cuts[c]], out_sem.at[c]) for c in order}
    for c in order:
        loads[c].start()
    for c in order:
        loads[c].wait()
        for i in range(c * step, (c + 1) * step):
            plane = wide[i].astype(BF16)
            narrow[i] = plane
            if i < 3:
                first[i] = plane
            if i >= STATIONS - 3:
                last[i - STATIONS + 3] = plane
        stores[c].start()
    for c in order:
        stores[c].wait()


def stencil_kernel(keep, take, velocity, register, eddy, low, high, base, offset):
    def plane(i):
        if i < 0:
            return low[i + 3].astype(F32)
        if i >= STATIONS:
            return high[i - STATIONS].astype(F32)
        return velocity[i]

    running = jnp.zeros((NY, WIDTH), F32)
    for i in range(STATIONS):
        here = velocity[i]
        total = (2.0 * coef_zero) * here
        for shift, coef in ((1, coef_one), (2, coef_two), (3, coef_three)):
            along = plane(i - shift) + plane(i + shift)
            across = pltpu.roll(here, shift, 0) + pltpu.roll(here, NY - shift, 0)
            total = total + coef * (along + across)
        part = decay * register[i] + eddy[i].astype(F32) * total
        base[i] = part
        running = keep[i] * running + take[i] * (here + weight * part)
    offset[...] = running


def span_kernel(lines, far_table, factor, _buffer, out, whole, table, scaled, held, line_sem, load_sem, sem):
    step = 256
    slabs = [pl.ds(n * step, step) for n in range(LENGTH // step)]
    loads = [
        pltpu.make_async_copy(far_table.at[:, cut], table.at[:, cut], load_sem.at[n]) for n, cut in enumerate(slabs)
    ]
    arrive = [
        pltpu.make_async_copy(lines.at[b], whole.at[:, pl.ds(b * WIDTH, WIDTH)], line_sem.at[b]) for b in range(PARTS)
    ]
    for copy in [*arrive, *loads]:
        copy.start()
    for copy in arrive:
        copy.wait()
    for n in range(LENGTH // step):
        loads[n].wait()
        cut = slice(n * step, (n + 1) * step)
        part = jnp.dot(whole[...], table[:, cut], preferred_element_type=F32)
        scaled[:, cut] = (part * factor[:, cut]).astype(BF16)
    blocks = [pl.ds(n * step // WIDTH, step // WIDTH) for n in range(LENGTH // step)]
    copies = [pltpu.make_async_copy(held.at[b], out.at[b], sem.at[n]) for n, b in enumerate(blocks)]
    for n in range(LENGTH // step):
        part = lax.dot_general(
            scaled[...],
            table[n * step : (n + 1) * step, :],
            (((1,), (1,)), ((), ())),
            preferred_element_type=F32,
        ).astype(BF16)
        for b in range(step // WIDTH):
            held[n * step // WIDTH + b] = part[:, b * WIDTH : (b + 1) * WIDTH]
        copies[n].start()
    for copy in copies:
        copy.wait()


def store_payload(out, plane, gain):
    upper = gain.astype(BF16).astype(F32)
    tail = jnp.concatenate([upper, gain - upper], axis=0).astype(BF16)
    plane = plane.astype(BF16)
    for m in range(4):
        out[m, 0:NY] = plane
        out[m, NY:PAYLOAD] = tail


def offset_kernel(keep, take, second, eddy, base_offset, out):
    running = jnp.zeros((NY, WIDTH), F32)
    gain = jnp.ones((8, WIDTH), F32)
    for i in range(STATIONS):
        term = eddy[i].astype(F32) * second[i].astype(F32)
        running = keep[i] * running + (take[i] * weight) * term
        gain = gain * keep[i]
    store_payload(out, running + base_offset[...], gain)


def local_kernel(keep, take, velocity, base, eddy, second, _, register, local, new_held, held, sem):
    step = STATIONS // CUTS
    cuts = [pl.ds(c * step, step) for c in range(CUTS)]
    copies = [
        (
            pltpu.make_async_copy(new_held.at[cuts[c]], register.at[cuts[c]], sem.at[0, c]),
            pltpu.make_async_copy(held.at[cuts[c]], local.at[cuts[c]], sem.at[1, c]),
        )
        for c in range(CUTS)
    ]
    running = jnp.zeros((NY, WIDTH), F32)
    for c in range(CUTS):
        for i in range(c * step, (c + 1) * step):
            new = base[i] + eddy[i].astype(F32) * second[i].astype(F32)
            new_held[i] = new
            running = keep[i] * running + take[i] * (velocity[i] + weight * new)
            held[i] = running
        for copy in copies[c]:
            copy.start()
    for pair in copies:
        for copy in pair:
            copy.wait()


def fold(place, received):
    total = jnp.zeros((NY, WIDTH), F32)
    gain = jnp.ones((8, WIDTH), F32)
    before, gain_before = total, gain
    for m in range(4):
        reached = place == m
        before = jnp.where(reached, total, before)
        gain_before = jnp.where(reached, gain, gain_before)
        tail = received[m, NY:PAYLOAD].astype(F32)
        one = tail[0:8] + tail[8:16]
        total = total * one[0:1] + received[m, 0:NY].astype(F32)
        gain = gain * one
    return before, gain_before, total, gain


def fold_kernel(place, received, before, gain_before, out):
    one, two, total, gain = fold(place[0], received)
    before[...] = one
    gain_before[...] = two
    store_payload(out, total, gain)


def final_kernel(
    place, keep, received, before1, gain1, before2, gain2, inflow, local, out, held, done, in_sem, out_sem
):
    step = STATIONS // CUTS
    cuts = [pl.ds(c * step, step) for c in range(CUTS)]
    loads = [pltpu.make_async_copy(local.at[cuts[c]], held.at[cuts[c]], in_sem.at[c]) for c in range(CUTS)]
    stores = [pltpu.make_async_copy(done.at[cuts[c]], out.at[cuts[c]], out_sem.at[c]) for c in range(CUTS)]
    for load in loads:
        load.start()
    before, gain, _, _ = fold(place[0], received)
    value = before + gain[0:1] * inflow[...]
    value = before2[...] + gain2[0:1] * value
    running = before1[...] + gain1[0:1] * value
    for c in range(CUTS):
        loads[c].wait()
        for i in range(c * step, (c + 1) * step):
            running = running * keep[i]
            done[i] = held[i] + running
        stores[c].start()
    for store in stores:
        store.wait()


SMEM = pl.BlockSpec(memory_space=pltpu.SMEM)
VMEM = pl.BlockSpec(memory_space=pltpu.VMEM)
ANY = pl.BlockSpec(memory_space=pl.ANY)
HBM = pl.BlockSpec(memory_space=pltpu.HBM)
CUBE = jax.ShapeDtypeStruct((STATIONS, NY, WIDTH), F32)
PLANE = jax.ShapeDtypeStruct((NY, WIDTH), F32)
GAIN = jax.ShapeDtypeStruct((8, WIDTH), F32)
EDGE = jax.ShapeDtypeStruct((3, NY, WIDTH), BF16)
DMA = pltpu.SemaphoreType.DMA
SLOTS = jax.ShapeDtypeStruct((4, PAYLOAD, WIDTH), BF16)


def call(kernel, name, in_specs, out_specs, out_shape, flops, bytes_accessed, scratch=(), limit=16, alias=None):
    return pl.pallas_call(
        kernel,
        name=name,
        in_specs=in_specs,
        out_specs=out_specs,
        out_shape=out_shape,
        scratch_shapes=scratch,
        input_output_aliases=alias or {},
        compiler_params=pltpu.CompilerParams(vmem_limit_bytes=int(limit * MIB)),
        cost_estimate=pl.CostEstimate(flops=flops, bytes_accessed=bytes_accessed, transcendentals=0),
    )


def body(velocity, register, eddy_viscosity, courant, inflow):
    table, factor = span_tables()
    place = lax.axis_index("gx")
    places = [jnp.reshape(p, (1,)) for p in (place % 4, place // 4 % 4, place // 16)]
    keep = courant / (1.0 + courant)
    take = 1.0 / (1.0 + courant)

    rounded, first, last = call(
        round_kernel,
        "round",
        [HBM],
        (HBM, VMEM, VMEM),
        (jax.ShapeDtypeStruct(CUBE.shape, BF16), EDGE, EDGE),
        300_000,
        1_600_000,
        (pltpu.VMEM(CUBE.shape, F32), pltpu.VMEM(CUBE.shape, BF16), DMA((CUTS,)), DMA((CUTS,))),
        LARGE,
    )(velocity)
    rounded = rounded.reshape(PARTS, ROWS, WIDTH)
    lines = lax.all_to_all(rounded, "gz", 0, 0, tiled=True)

    count = lax.axis_size("gx")
    forward = [(i, i + 1) for i in range(count - 1)]
    backward = [(b, a) for a, b in forward]
    low = lax.ppermute(last, "gx", forward)
    high = lax.ppermute(first, "gx", backward)
    lines, low, high = lax.optimization_barrier((lines, low, high))
    base, base_offset = call(
        stencil_kernel, "stencil", [SMEM, SMEM] + [VMEM] * 5, (VMEM, VMEM), (CUBE, PLANE), 8_000_000, 4_000_000
    )(keep, take, velocity, register, eddy_viscosity, low, high)

    derived = call(
        span_kernel,
        "span",
        [HBM, HBM, VMEM, HBM],
        HBM,
        jax.ShapeDtypeStruct((PARTS, ROWS, WIDTH), BF16),
        4 * ROWS * LENGTH * LENGTH,
        3_200_000,
        (
            pltpu.VMEM((ROWS, LENGTH), BF16),
            pltpu.VMEM((LENGTH, LENGTH), BF16),
            pltpu.VMEM((ROWS, LENGTH), BF16),
            pltpu.VMEM((PARTS, ROWS, WIDTH), BF16),
            DMA((PARTS,)),
            DMA((LENGTH // 256,)),
            DMA((LENGTH // 256,)),
        ),
        LARGE,
        {3: 0},
    )(lines, jnp.asarray(table), jnp.asarray(factor), rounded)
    second = lax.all_to_all(derived, "gz", 0, 0, tiled=True).reshape(STATIONS, NY, WIDTH)

    payload = call(offset_kernel, "offset", [SMEM, SMEM] + [VMEM] * 3, VMEM, SLOTS, 1_500_000, 1_100_000)(
        keep, take, second, eddy_viscosity, base_offset
    )
    new_register, local = call(
        local_kernel,
        "local",
        [SMEM, SMEM] + [VMEM] * 4 + [ANY],
        (HBM, HBM),
        (CUBE, CUBE),
        3_000_000,
        5_000_000,
        (pltpu.VMEM(CUBE.shape, F32), pltpu.VMEM(CUBE.shape, F32), DMA((2, CUTS))),
    )(keep, take, velocity, base, eddy_viscosity, second, payload)

    found = []
    for level in range(3):
        payload = lax.all_to_all(payload, "gx", 0, 0, axis_index_groups=GROUPS[level], tiled=True)
        if level < 2:
            before, gain, payload = call(
                fold_kernel, "fold", [SMEM, VMEM], (VMEM,) * 3, (PLANE, GAIN, SLOTS), 200_000, 300_000
            )(places[level], payload)
            found += [before, gain]

    new_velocity = call(
        final_kernel,
        "final",
        [SMEM, SMEM] + [VMEM] * 6 + [HBM],
        HBM,
        CUBE,
        800_000,
        2_300_000,
        (pltpu.VMEM(CUBE.shape, F32), pltpu.VMEM(CUBE.shape, F32), DMA((CUTS,)), DMA((CUTS,))),
        alias={8: 0},
    )(places[2], keep, payload, *found, inflow, local)
    return new_velocity, new_register


def solution(mesh):
    return jax.shard_map(
        body,
        mesh=mesh,
        in_specs=(
            P("gx", None, "gz"),
            P("gx", None, "gz"),
            P("gx", None, "gz"),
            P("gx"),
            P(None, "gz"),
        ),
        out_specs=(P("gx", None, "gz"), P("gx", None, "gz")),
        check_vma=False,
    )
```

```python
import math

import jax
import jax.numpy as jnp
import numpy as np
from jax import lax
from jax.experimental import pallas as pl
from jax.experimental.pallas import tpu as pltpu
from jax.sharding import PartitionSpec as P

coef_zero = -49.0 / 18.0
coef_one = 1.5
coef_two = -3.0 / 20.0
coef_three = 1.0 / 90.0
decay = -5.0 / 9.0
weight = 15.0 / 16.0

STATIONS, NY, WIDTH, PARTS = 32, 64, 128, 8
CUTS = 4
LENGTH = WIDTH * PARTS
ROWS = STATIONS * NY // PARTS
MIB = 1024 * 1024
SLABS = 4
LARGE = 62.75
F32, BF16 = jnp.float32, jnp.bfloat16
PAYLOAD = NY + 16

GROUPS = (
    [[x * 16 + h * 4 + l for l in range(4)] for x in range(4) for h in range(4)],
    [[x * 16 + h * 4 + l for h in range(4)] for x in range(4) for l in range(4)],
    [[x * 16 + z for x in range(4)] for z in range(16)],
)


def span_tables():
    position = np.arange(LENGTH, dtype=np.int64)
    product = position[:, None] * position[None, 1 : LENGTH // 2 + 1] % LENGTH
    angle = product.astype(np.float32) * np.float32(2.0 * math.pi / LENGTH)
    table = np.concatenate([np.cos(angle), np.sin(angle)], axis=1).astype(BF16)
    wave = np.arange(1, LENGTH // 2 + 1).astype(np.float32) * np.float32(2.0 * math.pi / LENGTH)
    factor = -(wave * wave) / np.float32(LENGTH)
    twice = np.where(np.arange(1, LENGTH // 2 + 1) < LENGTH // 2, 2.0, 1.0).astype(np.float32)
    factor = np.concatenate([factor * twice] * 2)[None, :].astype(np.float32)
    return table, factor


def stencil_kernel(keep, take, far_velocity, far_register, eddy, low, high, *rest):
    base, (offset, velocity, register, sem) = rest[:CUTS], rest[CUTS:]
    step = STATIONS // CUTS
    cuts = [pl.ds(c * step, step) for c in range(CUTS)]
    loads = [
        [
            pltpu.make_async_copy(far.at[cuts[c]], near.at[cuts[c]], sem.at[k, c])
            for c in range(CUTS)
        ]
        for k, (far, near) in enumerate(((far_velocity, velocity), (far_register, register)))
    ]
    for c in range(CUTS):
        loads[0][c].start()
        loads[1][c].start()

    def plane(i):
        if i < 0:
            return low[i + 3].astype(F32)
        if i >= STATIONS:
            return high[i - STATIONS].astype(F32)
        return velocity[i]

    running = jnp.zeros((NY, WIDTH), F32)
    loads[0][0].wait()
    for c in range(CUTS):
        if c + 1 < CUTS:
            loads[0][c + 1].wait()
        loads[1][c].wait()
        for i in range(c * step, (c + 1) * step):
            here = velocity[i]
            total = (2.0 * coef_zero) * here
            for shift, coef in ((1, coef_one), (2, coef_two), (3, coef_three)):
                along = plane(i - shift) + plane(i + shift)
                across = pltpu.roll(here, shift, 0) + pltpu.roll(here, NY - shift, 0)
                total = total + coef * (along + across)
            part = decay * register[i] + eddy[i].astype(F32) * total
            base[c][i - c * step] = part
            running = keep[i] * running + take[i] * (here + weight * part)
    offset[...] = running


def span_kernel(lines, factor, _buffer, *rest):
    slabs, out, scaled, held, sem = rest[:SLABS], *rest[SLABS:]
    step = LENGTH // SLABS
    whole = jnp.concatenate([lines[b] for b in range(PARTS)], axis=1)
    for n, slab in enumerate(slabs):
        part = jnp.dot(whole, slab[...], preferred_element_type=F32)
        scaled[n] = (part * factor[:, n * step : (n + 1) * step]).astype(BF16)
    wide = 256
    per = wide // WIDTH
    blocks = [pl.ds(n * per, per) for n in range(LENGTH // wide)]
    copies = [pltpu.make_async_copy(held.at[b], out.at[b], sem.at[n]) for n, b in enumerate(blocks)]
    for n in range(LENGTH // wide):
        part = jnp.zeros((ROWS, wide), F32)
        for m, slab in enumerate(slabs):
            part = part + lax.dot_general(
                scaled[m], slab[n * wide : (n + 1) * wide, :], (((1,), (1,)), ((), ())), preferred_element_type=F32
            )
        part = part.astype(BF16)
        for b in range(per):
            held[n * per + b] = part[:, b * WIDTH : (b + 1) * WIDTH]
        copies[n].start()
    for copy in copies:
        copy.wait()


def store_payload(out, plane, gain):
    upper = gain.astype(BF16).astype(F32)
    tail = jnp.concatenate([upper, gain - upper], axis=0).astype(BF16)
    plane = plane.astype(BF16)
    for m in range(4):
        out[m, 0:NY] = plane
        out[m, NY:PAYLOAD] = tail


def offset_kernel(keep, take, second, eddy, base_offset, out):
    running = jnp.zeros((NY, WIDTH), F32)
    gain = jnp.ones((8, WIDTH), F32)
    for i in range(STATIONS):
        term = eddy[i].astype(F32) * second[i].astype(F32)
        running = keep[i] * running + (take[i] * weight) * term
        gain = gain * keep[i]
    store_payload(out, running + base_offset[...], gain)


def local_kernel(keep, take, velocity, eddy, second, _, *rest):
    base, register, local, (held, sem) = rest[:CUTS], rest[CUTS], rest[CUTS + 1 : 2 * CUTS + 1], rest[2 * CUTS + 1 :]
    step = STATIONS // CUTS
    cuts = [pl.ds(c * step, step) for c in range(CUTS)]
    copies = [pltpu.make_async_copy(held.at[cuts[c]], register.at[cuts[c]], sem.at[c]) for c in range(CUTS)]
    running = jnp.zeros((NY, WIDTH), F32)
    for c in range(CUTS):
        for i in range(c * step, (c + 1) * step):
            new = base[c][i - c * step] + eddy[i].astype(F32) * second[i].astype(F32)
            held[i] = new
            running = keep[i] * running + take[i] * (velocity[i] + weight * new)
            local[c][i - c * step] = running
        copies[c].start()
    for copy in copies:
        copy.wait()


def fold(place, received):
    total = jnp.zeros((NY, WIDTH), F32)
    gain = jnp.ones((8, WIDTH), F32)
    before, gain_before = total, gain
    for m in range(4):
        reached = place == m
        before = jnp.where(reached, total, before)
        gain_before = jnp.where(reached, gain, gain_before)
        tail = received[m, NY:PAYLOAD].astype(F32)
        one = tail[0:8] + tail[8:16]
        total = total * one[0:1] + received[m, 0:NY].astype(F32)
        gain = gain * one
    return before, gain_before, total, gain


def fold_kernel(place, received, before, gain_before, out):
    one, two, total, gain = fold(place[0], received)
    before[...] = one
    gain_before[...] = two
    store_payload(out, total, gain)


def final_kernel(place, keep, received, before1, gain1, before2, gain2, inflow, *rest):
    local, out, done, sem = rest[:CUTS], rest[CUTS], rest[CUTS + 1], rest[CUTS + 2]
    step = STATIONS // CUTS
    cuts = [pl.ds(c * step, step) for c in range(CUTS)]
    stores = [pltpu.make_async_copy(done.at[cuts[c]], out.at[cuts[c]], sem.at[c]) for c in range(CUTS)]
    before, gain, _, _ = fold(place[0], received)
    value = before + gain[0:1] * inflow[...]
    value = before2[...] + gain2[0:1] * value
    running = before1[...] + gain1[0:1] * value
    for c in range(CUTS):
        for i in range(step):
            running = running * keep[c * step + i]
            done[c * step + i] = local[c][i] + running
        stores[c].start()
    for store in stores:
        store.wait()


SMEM = pl.BlockSpec(memory_space=pltpu.SMEM)
VMEM = pl.BlockSpec(memory_space=pltpu.VMEM)
ANY = pl.BlockSpec(memory_space=pl.ANY)
HBM = pl.BlockSpec(memory_space=pltpu.HBM)
CUBE = jax.ShapeDtypeStruct((STATIONS, NY, WIDTH), F32)
PLANE = jax.ShapeDtypeStruct((NY, WIDTH), F32)
GAIN = jax.ShapeDtypeStruct((8, WIDTH), F32)
PART = jax.ShapeDtypeStruct((STATIONS // CUTS, NY, WIDTH), F32)
EDGE = jax.ShapeDtypeStruct((3, NY, WIDTH), BF16)
DMA = pltpu.SemaphoreType.DMA
SLOTS = jax.ShapeDtypeStruct((4, PAYLOAD, WIDTH), BF16)


def call(kernel, name, in_specs, out_specs, out_shape, flops, bytes_accessed, scratch=(), limit=16, alias=None):
    return pl.pallas_call(
        kernel,
        name=name,
        in_specs=in_specs,
        out_specs=out_specs,
        out_shape=out_shape,
        scratch_shapes=scratch,
        input_output_aliases=alias or {},
        compiler_params=pltpu.CompilerParams(vmem_limit_bytes=int(limit * MIB)),
        cost_estimate=pl.CostEstimate(flops=flops, bytes_accessed=bytes_accessed, transcendentals=0),
    )


def body(velocity, register, eddy_viscosity, courant, inflow):
    table, factor = span_tables()
    place = lax.axis_index("gx")
    places = [jnp.reshape(p, (1,)) for p in (place % 4, place // 4 % 4, place // 16)]
    keep = courant / (1.0 + courant)
    take = 1.0 / (1.0 + courant)

    rounded = velocity.astype(BF16)
    first, last = velocity[:3].astype(BF16), velocity[STATIONS - 3 :].astype(BF16)
    rounded = rounded.reshape(PARTS, ROWS, WIDTH)
    lines = lax.all_to_all(rounded, "gz", 0, 0, tiled=True)

    count = lax.axis_size("gx")
    forward = [(i, i + 1) for i in range(count - 1)]
    backward = [(b, a) for a, b in forward]
    low = lax.ppermute(last, "gx", forward)
    high = lax.ppermute(first, "gx", backward)
    lines, low, high = lax.optimization_barrier((lines, low, high))
    *base, base_offset = call(
        stencil_kernel,
        "stencil",
        [SMEM, SMEM, HBM, HBM] + [VMEM] * 3,
        (VMEM,) * (CUTS + 1),
        (PART,) * CUTS + (PLANE,),
        8_000_000,
        4_000_000,
        (pltpu.VMEM(CUBE.shape, F32), pltpu.VMEM(CUBE.shape, F32), DMA((2, CUTS))),
        LARGE,
    )(keep, take, velocity, register, eddy_viscosity, low, high)

    step = LENGTH // SLABS
    slabs = [jnp.asarray(table[:, n * step : (n + 1) * step]) for n in range(SLABS)]
    derived = call(
        span_kernel,
        "span",
        [VMEM, VMEM, HBM] + [VMEM] * SLABS,
        HBM,
        jax.ShapeDtypeStruct((PARTS, ROWS, WIDTH), BF16),
        4 * ROWS * LENGTH * LENGTH,
        3_200_000,
        (
            pltpu.VMEM((SLABS, ROWS, step), BF16),
            pltpu.VMEM((PARTS, ROWS, WIDTH), BF16),
            DMA((LENGTH // 256,)),
        ),
        alias={2: 0},
    )(lines, jnp.asarray(factor), rounded, *slabs)
    second = lax.all_to_all(derived, "gz", 0, 0, tiled=True).reshape(STATIONS, NY, WIDTH)

    payload = call(offset_kernel, "offset", [SMEM, SMEM] + [VMEM] * 3, VMEM, SLOTS, 1_500_000, 1_100_000)(
        keep, take, second, eddy_viscosity, base_offset
    )
    new_register, *local = call(
        local_kernel,
        "local",
        [SMEM, SMEM] + [VMEM] * 3 + [ANY] + [VMEM] * CUTS,
        (HBM,) + (VMEM,) * CUTS,
        (CUBE,) + (PART,) * CUTS,
        3_000_000,
        5_000_000,
        (pltpu.VMEM(CUBE.shape, F32), DMA((CUTS,))),
        alias={6 + c: 1 + c for c in range(CUTS)},
    )(keep, take, velocity, eddy_viscosity, second, payload, *base)

    found = []
    for level in range(3):
        payload = lax.all_to_all(payload, "gx", 0, 0, axis_index_groups=GROUPS[level], tiled=True)
        if level < 2:
            before, gain, payload = call(
                fold_kernel, "fold", [SMEM, VMEM], (VMEM,) * 3, (PLANE, GAIN, SLOTS), 200_000, 300_000
            )(places[level], payload)
            found += [before, gain]

    new_velocity = call(
        final_kernel,
        "final",
        [SMEM, SMEM] + [VMEM] * (6 + CUTS),
        HBM,
        CUBE,
        800_000,
        2_300_000,
        (pltpu.VMEM(CUBE.shape, F32), DMA((CUTS,))),
    )(places[2], keep, payload, *found, inflow, *local)
    return new_velocity, new_register


def solution(mesh):
    return jax.shard_map(
        body,
        mesh=mesh,
        in_specs=(
            P("gx", None, "gz"),
            P("gx", None, "gz"),
            P("gx", None, "gz"),
            P("gx"),
            P(None, "gz"),
        ),
        out_specs=(P("gx", None, "gz"), P("gx", None, "gz")),
        check_vma=False,
    )
```

```python
import math

import jax
import jax.numpy as jnp
import numpy as np
from jax import lax
from jax.experimental import pallas as pl
from jax.experimental.pallas import tpu as pltpu
from jax.sharding import PartitionSpec as P

coef_zero = -49.0 / 18.0
coef_one = 1.5
coef_two = -3.0 / 20.0
coef_three = 1.0 / 90.0
decay = -5.0 / 9.0
weight = 15.0 / 16.0

STATIONS, NY, WIDTH, PARTS = 32, 64, 128, 8
CUTS = 4
LENGTH = WIDTH * PARTS
ROWS = STATIONS * NY // PARTS
MIB = 1024 * 1024
SLABS = 4
LARGE = 62.5
F32, BF16 = jnp.float32, jnp.bfloat16
PAYLOAD = NY + 16

GROUPS = (
    [[x * 16 + h * 4 + l for l in range(4)] for x in range(4) for h in range(4)],
    [[x * 16 + h * 4 + l for h in range(4)] for x in range(4) for l in range(4)],
    [[x * 16 + z for x in range(4)] for z in range(16)],
)


def span_tables():
    position = np.arange(LENGTH, dtype=np.int64)
    product = position[:, None] * position[None, 1 : LENGTH // 2 + 1] % LENGTH
    angle = product.astype(np.float32) * np.float32(2.0 * math.pi / LENGTH)
    table = np.concatenate([np.cos(angle), np.sin(angle)], axis=1).astype(BF16)
    wave = np.arange(1, LENGTH // 2 + 1).astype(np.float32) * np.float32(2.0 * math.pi / LENGTH)
    factor = -(wave * wave) / np.float32(LENGTH)
    twice = np.where(np.arange(1, LENGTH // 2 + 1) < LENGTH // 2, 2.0, 1.0).astype(np.float32)
    factor = np.concatenate([factor * twice] * 2)[None, :].astype(np.float32)
    return table, factor


def edge_kernel(rounded, first, last, sem):
    copies = [
        pltpu.make_async_copy(rounded.at[pl.ds(0, 3)], first, sem.at[0]),
        pltpu.make_async_copy(rounded.at[pl.ds(STATIONS - 3, 3)], last, sem.at[1]),
    ]
    for copy in copies:
        copy.start()
    for copy in copies:
        copy.wait()


def stencil_kernel(keep, take, far_velocity, far_register, eddy, low, high, *rest):
    base, (offset, velocity, register, sem) = rest[:CUTS], rest[CUTS:]
    step = STATIONS // CUTS
    cuts = [pl.ds(c * step, step) for c in range(CUTS)]
    loads = [
        [
            pltpu.make_async_copy(far.at[cuts[c]], near.at[cuts[c]], sem.at[k, c])
            for c in range(CUTS)
        ]
        for k, (far, near) in enumerate(((far_velocity, velocity), (far_register, register)))
    ]
    for c in range(CUTS):
        loads[0][c].start()
        loads[1][c].start()

    def plane(i):
        if i < 0:
            return low[i + 3].astype(F32)
        if i >= STATIONS:
            return high[i - STATIONS].astype(F32)
        return velocity[i]

    running = jnp.zeros((NY, WIDTH), F32)
    loads[0][0].wait()
    for c in range(CUTS):
        if c + 1 < CUTS:
            loads[0][c + 1].wait()
        loads[1][c].wait()
        for i in range(c * step, (c + 1) * step):
            here = velocity[i]
            total = (2.0 * coef_zero) * here
            for shift, coef in ((1, coef_one), (2, coef_two), (3, coef_three)):
                along = plane(i - shift) + plane(i + shift)
                across = pltpu.roll(here, shift, 0) + pltpu.roll(here, NY - shift, 0)
                total = total + coef * (along + across)
            part = decay * register[i] + eddy[i].astype(F32) * total
            base[c][i - c * step] = part
            running = keep[i] * running + take[i] * (here + weight * part)
    offset[...] = running


def span_kernel(lines, factor, _buffer, *rest):
    slabs, out, scaled, held, sem = rest[:SLABS], *rest[SLABS:]
    step = LENGTH // SLABS
    whole = jnp.concatenate([lines[b] for b in range(PARTS)], axis=1)
    for n, slab in enumerate(slabs):
        part = jnp.dot(whole, slab[...], preferred_element_type=F32)
        scaled[n] = (part * factor[:, n * step : (n + 1) * step]).astype(BF16)
    wide = 256
    per = wide // WIDTH
    blocks = [pl.ds(n * per, per) for n in range(LENGTH // wide)]
    copies = [pltpu.make_async_copy(held.at[b], out.at[b], sem.at[n]) for n, b in enumerate(blocks)]
    for n in range(LENGTH // wide):
        part = jnp.zeros((ROWS, wide), F32)
        for m, slab in enumerate(slabs):
            part = part + lax.dot_general(
                scaled[m], slab[n * wide : (n + 1) * wide, :], (((1,), (1,)), ((), ())), preferred_element_type=F32
            )
        part = part.astype(BF16)
        for b in range(per):
            held[n * per + b] = part[:, b * WIDTH : (b + 1) * WIDTH]
        copies[n].start()
    for copy in copies:
        copy.wait()


def store_payload(out, plane, gain):
    upper = gain.astype(BF16).astype(F32)
    tail = jnp.concatenate([upper, gain - upper], axis=0).astype(BF16)
    plane = plane.astype(BF16)
    for m in range(4):
        out[m, 0:NY] = plane
        out[m, NY:PAYLOAD] = tail


def offset_kernel(keep, take, second, eddy, base_offset, out):
    running = jnp.zeros((NY, WIDTH), F32)
    gain = jnp.ones((8, WIDTH), F32)
    for i in range(STATIONS):
        term = eddy[i].astype(F32) * second[i].astype(F32)
        running = keep[i] * running + (take[i] * weight) * term
        gain = gain * keep[i]
    store_payload(out, running + base_offset[...], gain)


def local_kernel(keep, take, velocity, eddy, second, _, *rest):
    base, register, local, (held, sem) = rest[:CUTS], rest[CUTS], rest[CUTS + 1 : 2 * CUTS + 1], rest[2 * CUTS + 1 :]
    step = STATIONS // CUTS
    cuts = [pl.ds(c * step, step) for c in range(CUTS)]
    copies = [pltpu.make_async_copy(held.at[cuts[c]], register.at[cuts[c]], sem.at[c]) for c in range(CUTS)]
    running = jnp.zeros((NY, WIDTH), F32)
    for c in range(CUTS):
        for i in range(c * step, (c + 1) * step):
            new = base[c][i - c * step] + eddy[i].astype(F32) * second[i].astype(F32)
            held[i] = new
            running = keep[i] * running + take[i] * (velocity[i] + weight * new)
            local[c][i - c * step] = running
        copies[c].start()
    for copy in copies:
        copy.wait()


def hold_kernel(plane, held):
    held[...] = plane[...]


def fold(place, received):
    total = jnp.zeros((NY, WIDTH), F32)
    gain = jnp.ones((8, WIDTH), F32)
    before, gain_before = total, gain
    for m in range(4):
        reached = place == m
        before = jnp.where(reached, total, before)
        gain_before = jnp.where(reached, gain, gain_before)
        tail = received[m, NY:PAYLOAD].astype(F32)
        one = tail[0:8] + tail[8:16]
        total = total * one[0:1] + received[m, 0:NY].astype(F32)
        gain = gain * one
    return before, gain_before, total, gain


def fold_kernel(place, received, *rest):
    before, gain_before, out = rest[-3:]
    one, two, total, gain = fold(place[0], received)
    before[...] = one
    gain_before[...] = two
    store_payload(out, total, gain)


def final_kernel(place, keep, received, before1, gain1, before2, gain2, inflow, *rest):
    local, out, done, sem = rest[:CUTS], rest[CUTS], rest[CUTS + 1], rest[CUTS + 2]
    step = STATIONS // CUTS
    cuts = [pl.ds(c * step, step) for c in range(CUTS)]
    stores = [pltpu.make_async_copy(done.at[cuts[c]], out.at[cuts[c]], sem.at[c]) for c in range(CUTS)]
    before, gain, _, _ = fold(place[0], received)
    value = before + gain[0:1] * inflow[...]
    value = before2[...] + gain2[0:1] * value
    running = before1[...] + gain1[0:1] * value
    for c in range(CUTS):
        for i in range(step):
            running = running * keep[c * step + i]
            done[c * step + i] = local[c][i] + running
        stores[c].start()
    for store in stores:
        store.wait()


SMEM = pl.BlockSpec(memory_space=pltpu.SMEM)
VMEM = pl.BlockSpec(memory_space=pltpu.VMEM)
ANY = pl.BlockSpec(memory_space=pl.ANY)
HBM = pl.BlockSpec(memory_space=pltpu.HBM)
CUBE = jax.ShapeDtypeStruct((STATIONS, NY, WIDTH), F32)
PLANE = jax.ShapeDtypeStruct((NY, WIDTH), F32)
GAIN = jax.ShapeDtypeStruct((8, WIDTH), F32)
PART = jax.ShapeDtypeStruct((STATIONS // CUTS, NY, WIDTH), F32)
EDGE = jax.ShapeDtypeStruct((3, NY, WIDTH), BF16)
DMA = pltpu.SemaphoreType.DMA
SLOTS = jax.ShapeDtypeStruct((4, PAYLOAD, WIDTH), BF16)


def call(kernel, name, in_specs, out_specs, out_shape, flops, bytes_accessed, scratch=(), limit=16, alias=None):
    return pl.pallas_call(
        kernel,
        name=name,
        in_specs=in_specs,
        out_specs=out_specs,
        out_shape=out_shape,
        scratch_shapes=scratch,
        input_output_aliases=alias or {},
        compiler_params=pltpu.CompilerParams(vmem_limit_bytes=int(limit * MIB)),
        cost_estimate=pl.CostEstimate(flops=flops, bytes_accessed=bytes_accessed, transcendentals=0),
    )


def body(velocity, register, eddy_viscosity, courant, inflow):
    table, factor = span_tables()
    place = lax.axis_index("gx")
    places = [jnp.reshape(p, (1,)) for p in (place % 4, place // 4 % 4, place // 16)]
    keep = courant / (1.0 + courant)
    take = 1.0 / (1.0 + courant)

    rounded = velocity.astype(BF16)
    first, last = call(edge_kernel, "edge", [HBM], (VMEM, VMEM), (EDGE, EDGE), 3_000_000_000, 200_000, (DMA((2,)),))(rounded)
    rounded = rounded.reshape(PARTS, ROWS, WIDTH)
    lines = lax.all_to_all(rounded, "gz", 0, 0, tiled=True)

    count = lax.axis_size("gx")
    forward = [(i, i + 1) for i in range(count - 1)]
    backward = [(b, a) for a, b in forward]
    low = lax.ppermute(last, "gx", forward)
    high = lax.ppermute(first, "gx", backward)
    lines, low, high = lax.optimization_barrier((lines, low, high))
    *base, base_offset = call(
        stencil_kernel,
        "stencil",
        [SMEM, SMEM, HBM, HBM] + [VMEM] * 3,
        (VMEM,) * (CUTS + 1),
        (PART,) * CUTS + (PLANE,),
        8_000_000,
        4_000_000,
        (pltpu.VMEM(CUBE.shape, F32), pltpu.VMEM(CUBE.shape, F32), DMA((2, CUTS))),
        LARGE,
    )(keep, take, velocity, register, eddy_viscosity, low, high)

    base_offset = call(hold_kernel, "hold", [VMEM], VMEM, PLANE, 1000, 100_000)(base_offset)

    step = LENGTH // SLABS
    slabs = [jnp.asarray(table[:, n * step : (n + 1) * step]) for n in range(SLABS)]
    derived = call(
        span_kernel,
        "span",
        [VMEM, VMEM, HBM] + [VMEM] * SLABS,
        HBM,
        jax.ShapeDtypeStruct((PARTS, ROWS, WIDTH), BF16),
        4 * ROWS * LENGTH * LENGTH,
        3_200_000,
        (
            pltpu.VMEM((SLABS, ROWS, step), BF16),
            pltpu.VMEM((PARTS, ROWS, WIDTH), BF16),
            DMA((LENGTH // 256,)),
        ),
        alias={2: 0},
    )(lines, jnp.asarray(factor), rounded, *slabs)
    second = lax.all_to_all(derived, "gz", 0, 0, tiled=True).reshape(STATIONS, NY, WIDTH)

    payload = call(offset_kernel, "offset", [SMEM, SMEM] + [VMEM] * 3, VMEM, SLOTS, 1_500_000, 1_100_000)(
        keep, take, second, eddy_viscosity, base_offset
    )
    new_register, *local = call(
        local_kernel,
        "local",
        [SMEM, SMEM] + [VMEM] * 3 + [ANY] + [VMEM] * CUTS,
        (HBM,) + (VMEM,) * CUTS,
        (CUBE,) + (PART,) * CUTS,
        3_000_000,
        5_000_000,
        (pltpu.VMEM(CUBE.shape, F32), DMA((CUTS,))),
        alias={6 + c: 1 + c for c in range(CUTS)},
    )(keep, take, velocity, eddy_viscosity, second, payload, *base)

    found = []
    for level in range(3):
        payload = lax.all_to_all(payload, "gx", 0, 0, axis_index_groups=GROUPS[level], tiled=True)
        if level < 2:
            before, gain, payload = call(
                fold_kernel, "fold", [SMEM, VMEM] + [ANY] * level, (VMEM,) * 3, (PLANE, GAIN, SLOTS), 200_000, 300_000
            )(places[level], payload, *local[:level])
            found += [before, gain]

    new_velocity = call(
        final_kernel,
        "final",
        [SMEM, SMEM] + [VMEM] * (6 + CUTS),
        HBM,
        CUBE,
        800_000,
        2_300_000,
        (pltpu.VMEM(CUBE.shape, F32), DMA((CUTS,))),
    )(places[2], keep, payload, *found, inflow, *local)
    return new_velocity, new_register


def solution(mesh):
    return jax.shard_map(
        body,
        mesh=mesh,
        in_specs=(
            P("gx", None, "gz"),
            P("gx", None, "gz"),
            P("gx", None, "gz"),
            P("gx"),
            P(None, "gz"),
        ),
        out_specs=(P("gx", None, "gz"), P("gx", None, "gz")),
        check_vma=False,
    )
```

```python
import math

import jax
import jax.numpy as jnp
import numpy as np
from jax import lax
from jax.experimental import pallas as pl
from jax.experimental.pallas import tpu as pltpu
from jax.sharding import PartitionSpec as P

coef_zero = -49.0 / 18.0
coef_one = 1.5
coef_two = -3.0 / 20.0
coef_three = 1.0 / 90.0
decay = -5.0 / 9.0
weight = 15.0 / 16.0

STATIONS, NY, WIDTH, PARTS = 32, 64, 128, 8
CUTS = 4
LENGTH = WIDTH * PARTS
ROWS = STATIONS * NY // PARTS
MIB = 1024 * 1024
SLABS = 4
LARGE = 62.75
F32, BF16 = jnp.float32, jnp.bfloat16
PAYLOAD = NY + 16

GROUPS = (
    [[x * 16 + h * 4 + l for l in range(4)] for x in range(4) for h in range(4)],
    [[x * 16 + h * 4 + l for h in range(4)] for x in range(4) for l in range(4)],
    [[x * 16 + z for x in range(4)] for z in range(16)],
)


def span_tables():
    position = np.arange(LENGTH, dtype=np.int64)
    product = position[:, None] * position[None, 1 : LENGTH // 2 + 1] % LENGTH
    angle = product.astype(np.float32) * np.float32(2.0 * math.pi / LENGTH)
    table = np.concatenate([np.cos(angle), np.sin(angle)], axis=1).astype(BF16)
    wave = np.arange(1, LENGTH // 2 + 1).astype(np.float32) * np.float32(2.0 * math.pi / LENGTH)
    factor = -(wave * wave) / np.float32(LENGTH)
    twice = np.where(np.arange(1, LENGTH // 2 + 1) < LENGTH // 2, 2.0, 1.0).astype(np.float32)
    factor = np.concatenate([factor * twice] * 2)[None, :].astype(np.float32)
    return table, factor


def edge_kernel(rounded, first, last, sem):
    copies = [
        pltpu.make_async_copy(rounded.at[pl.ds(0, 3)], first, sem.at[0]),
        pltpu.make_async_copy(rounded.at[pl.ds(STATIONS - 3, 3)], last, sem.at[1]),
    ]
    for copy in copies:
        copy.start()
    for copy in copies:
        copy.wait()


def stencil_kernel(keep, take, far_velocity, far_register, eddy, low, high, *rest):
    base, (offset, velocity, register, sem) = rest[:CUTS], rest[CUTS:]
    step = STATIONS // CUTS
    cuts = [pl.ds(c * step, step) for c in range(CUTS)]
    loads = [
        [
            pltpu.make_async_copy(far.at[cuts[c]], near.at[cuts[c]], sem.at[k, c])
            for c in range(CUTS)
        ]
        for k, (far, near) in enumerate(((far_velocity, velocity), (far_register, register)))
    ]
    for c in range(CUTS):
        loads[0][c].start()
        loads[1][c].start()

    def plane(i):
        if i < 0:
            return low[i + 3].astype(F32)
        if i >= STATIONS:
            return high[i - STATIONS].astype(F32)
        return velocity[i]

    running = jnp.zeros((NY, WIDTH), F32)
    loads[0][0].wait()
    for c in range(CUTS):
        if c + 1 < CUTS:
            loads[0][c + 1].wait()
        loads[1][c].wait()
        for i in range(c * step, (c + 1) * step):
            here = velocity[i]
            total = (2.0 * coef_zero) * here
            for shift, coef in ((1, coef_one), (2, coef_two), (3, coef_three)):
                along = plane(i - shift) + plane(i + shift)
                across = pltpu.roll(here, shift, 0) + pltpu.roll(here, NY - shift, 0)
                total = total + coef * (along + across)
            part = decay * register[i] + eddy[i].astype(F32) * total
            base[c][i - c * step] = part
            running = keep[i] * running + take[i] * (here + weight * part)
    offset[...] = running


def span_kernel(lines, factor, _buffer, *rest):
    slabs, out, scaled, held, sem = rest[:SLABS], *rest[SLABS:]
    step = LENGTH // SLABS
    whole = jnp.concatenate([lines[b] for b in range(PARTS)], axis=1)
    for n, slab in enumerate(slabs):
        part = jnp.dot(whole, slab[...], preferred_element_type=F32)
        scaled[n] = (part * factor[:, n * step : (n + 1) * step]).astype(BF16)
    wide = 256
    per = wide // WIDTH
    blocks = [pl.ds(n * per, per) for n in range(LENGTH // wide)]
    copies = [pltpu.make_async_copy(held.at[b], out.at[b], sem.at[n]) for n, b in enumerate(blocks)]
    for n in range(LENGTH // wide):
        part = jnp.zeros((ROWS, wide), F32)
        for m, slab in enumerate(slabs):
            part = part + lax.dot_general(
                scaled[m], slab[n * wide : (n + 1) * wide, :], (((1,), (1,)), ((), ())), preferred_element_type=F32
            )
        part = part.astype(BF16)
        for b in range(per):
            held[n * per + b] = part[:, b * WIDTH : (b + 1) * WIDTH]
        copies[n].start()
    for copy in copies:
        copy.wait()


def store_payload(out, plane, gain):
    upper = gain.astype(BF16).astype(F32)
    tail = jnp.concatenate([upper, gain - upper], axis=0).astype(BF16)
    plane = plane.astype(BF16)
    for m in range(4):
        out[m, 0:NY] = plane
        out[m, NY:PAYLOAD] = tail


def offset_kernel(keep, take, second, eddy, base_offset, out):
    running = jnp.zeros((NY, WIDTH), F32)
    gain = jnp.ones((8, WIDTH), F32)
    for i in range(STATIONS):
        term = eddy[i].astype(F32) * second[i].astype(F32)
        running = keep[i] * running + (take[i] * weight) * term
        gain = gain * keep[i]
    store_payload(out, running + base_offset[...], gain)


def local_kernel(keep, take, velocity, eddy, second, _, *rest):
    base, register, local, (held, sem) = rest[:CUTS], rest[CUTS], rest[CUTS + 1 : 2 * CUTS + 1], rest[2 * CUTS + 1 :]
    step = STATIONS // CUTS
    cuts = [pl.ds(c * step, step) for c in range(CUTS)]
    copies = [pltpu.make_async_copy(held.at[cuts[c]], register.at[cuts[c]], sem.at[c]) for c in range(CUTS)]
    running = jnp.zeros((NY, WIDTH), F32)
    for c in range(CUTS):
        for i in range(c * step, (c + 1) * step):
            new = base[c][i - c * step] + eddy[i].astype(F32) * second[i].astype(F32)
            held[i] = new
            running = keep[i] * running + take[i] * (velocity[i] + weight * new)
            local[c][i - c * step] = running
        copies[c].start()
    for copy in copies:
        copy.wait()


def hold_kernel(plane, held):
    held[...] = plane[...]


def fold(place, received):
    total = jnp.zeros((NY, WIDTH), F32)
    gain = jnp.ones((8, WIDTH), F32)
    before, gain_before = total, gain
    for m in range(4):
        reached = place == m
        before = jnp.where(reached, total, before)
        gain_before = jnp.where(reached, gain, gain_before)
        tail = received[m, NY:PAYLOAD].astype(F32)
        one = tail[0:8] + tail[8:16]
        total = total * one[0:1] + received[m, 0:NY].astype(F32)
        gain = gain * one
    return before, gain_before, total, gain


def fold_kernel(place, received, before, gain_before, out):
    one, two, total, gain = fold(place[0], received)
    before[...] = one
    gain_before[...] = two
    store_payload(out, total, gain)


def final_kernel(place, keep, received, before1, gain1, before2, gain2, inflow, *rest):
    local, out, done, sem = rest[:CUTS], rest[CUTS], rest[CUTS + 1], rest[CUTS + 2]
    step = STATIONS // CUTS
    cuts = [pl.ds(c * step, step) for c in range(CUTS)]
    stores = [pltpu.make_async_copy(done.at[cuts[c]], out.at[cuts[c]], sem.at[c]) for c in range(CUTS)]
    before, gain, _, _ = fold(place[0], received)
    value = before + gain[0:1] * inflow[...]
    value = before2[...] + gain2[0:1] * value
    running = before1[...] + gain1[0:1] * value
    for c in range(CUTS):
        for i in range(step):
            running = running * keep[c * step + i]
            done[c * step + i] = local[c][i] + running
        stores[c].start()
    for store in stores:
        store.wait()


SMEM = pl.BlockSpec(memory_space=pltpu.SMEM)
VMEM = pl.BlockSpec(memory_space=pltpu.VMEM)
ANY = pl.BlockSpec(memory_space=pl.ANY)
HBM = pl.BlockSpec(memory_space=pltpu.HBM)
CUBE = jax.ShapeDtypeStruct((STATIONS, NY, WIDTH), F32)
PLANE = jax.ShapeDtypeStruct((NY, WIDTH), F32)
GAIN = jax.ShapeDtypeStruct((8, WIDTH), F32)
PART = jax.ShapeDtypeStruct((STATIONS // CUTS, NY, WIDTH), F32)
EDGE = jax.ShapeDtypeStruct((3, NY, WIDTH), BF16)
DMA = pltpu.SemaphoreType.DMA
SLOTS = jax.ShapeDtypeStruct((4, PAYLOAD, WIDTH), BF16)


def call(kernel, name, in_specs, out_specs, out_shape, flops, bytes_accessed, scratch=(), limit=16, alias=None):
    return pl.pallas_call(
        kernel,
        name=name,
        in_specs=in_specs,
        out_specs=out_specs,
        out_shape=out_shape,
        scratch_shapes=scratch,
        input_output_aliases=alias or {},
        compiler_params=pltpu.CompilerParams(vmem_limit_bytes=int(limit * MIB)),
        cost_estimate=pl.CostEstimate(flops=flops, bytes_accessed=bytes_accessed, transcendentals=0),
    )


def body(velocity, register, eddy_viscosity, courant, inflow):
    table, factor = span_tables()
    place = lax.axis_index("gx")
    places = [jnp.reshape(p, (1,)) for p in (place % 4, place // 4 % 4, place // 16)]
    keep = courant / (1.0 + courant)
    take = 1.0 / (1.0 + courant)

    rounded = velocity.astype(BF16)
    first, last = call(edge_kernel, "edge", [HBM], (VMEM, VMEM), (EDGE, EDGE), 3_000_000_000, 200_000, (DMA((2,)),))(rounded)
    rounded = rounded.reshape(PARTS, ROWS, WIDTH)
    lines = lax.all_to_all(rounded, "gz", 0, 0, tiled=True)

    count = lax.axis_size("gx")
    forward = [(i, i + 1) for i in range(count - 1)]
    backward = [(b, a) for a, b in forward]
    low = lax.ppermute(last, "gx", forward)
    high = lax.ppermute(first, "gx", backward)
    lines, low, high = lax.optimization_barrier((lines, low, high))
    *base, base_offset = call(
        stencil_kernel,
        "stencil",
        [SMEM, SMEM, HBM, HBM] + [VMEM] * 3,
        (VMEM,) * (CUTS + 1),
        (PART,) * CUTS + (PLANE,),
        8_000_000,
        4_000_000,
        (pltpu.VMEM(CUBE.shape, F32), pltpu.VMEM(CUBE.shape, F32), DMA((2, CUTS))),
        LARGE,
    )(keep, take, velocity, register, eddy_viscosity, low, high)

    base_offset = call(hold_kernel, "hold", [VMEM], VMEM, PLANE, 1000, 100_000)(base_offset)

    step = LENGTH // SLABS
    slabs = [jnp.asarray(table[:, n * step : (n + 1) * step]) for n in range(SLABS)]
    derived = call(
        span_kernel,
        "span",
        [VMEM, VMEM, HBM] + [VMEM] * SLABS,
        HBM,
        jax.ShapeDtypeStruct((PARTS, ROWS, WIDTH), BF16),
        4 * ROWS * LENGTH * LENGTH,
        3_200_000,
        (
            pltpu.VMEM((SLABS, ROWS, step), BF16),
            pltpu.VMEM((PARTS, ROWS, WIDTH), BF16),
            DMA((LENGTH // 256,)),
        ),
        alias={2: 0},
    )(lines, jnp.asarray(factor), rounded, *slabs)
    second = lax.all_to_all(derived, "gz", 0, 0, tiled=True).reshape(STATIONS, NY, WIDTH)

    payload = call(offset_kernel, "offset", [SMEM, SMEM] + [VMEM] * 3, VMEM, SLOTS, 1_500_000, 1_100_000)(
        keep, take, second, eddy_viscosity, base_offset
    )
    new_register, *local = call(
        local_kernel,
        "local",
        [SMEM, SMEM] + [VMEM] * 3 + [ANY] + [VMEM] * CUTS,
        (HBM,) + (VMEM,) * CUTS,
        (CUBE,) + (PART,) * CUTS,
        3_000_000,
        5_000_000,
        (pltpu.VMEM(CUBE.shape, F32), DMA((CUTS,))),
        alias={6 + c: 1 + c for c in range(CUTS)},
    )(keep, take, velocity, eddy_viscosity, second, payload, *base)

    found = []
    for level in range(3):
        payload = lax.all_to_all(payload, "gx", 0, 0, axis_index_groups=GROUPS[level], tiled=True)
        if level < 2:
            before, gain, payload = call(
                fold_kernel, "fold", [SMEM, VMEM], (VMEM,) * 3, (PLANE, GAIN, SLOTS), 200_000, 300_000
            )(places[level], payload)
            found += [before, gain]

    new_velocity = call(
        final_kernel,
        "final",
        [SMEM, SMEM] + [VMEM] * (6 + CUTS),
        HBM,
        CUBE,
        800_000,
        2_300_000,
        (pltpu.VMEM(CUBE.shape, F32), DMA((CUTS,))),
    )(places[2], keep, payload, *found, inflow, *local)
    return new_velocity, new_register


def solution(mesh):
    return jax.shard_map(
        body,
        mesh=mesh,
        in_specs=(
            P("gx", None, "gz"),
            P("gx", None, "gz"),
            P("gx", None, "gz"),
            P("gx"),
            P(None, "gz"),
        ),
        out_specs=(P("gx", None, "gz"), P("gx", None, "gz")),
        check_vma=False,
    )
```

```python
import functools
import math

import jax
import jax.numpy as jnp
import numpy as np
from jax import lax
from jax.experimental import pallas as pl
from jax.experimental.pallas import tpu as pltpu
from jax.sharding import PartitionSpec as P

coef_zero = -49.0 / 18.0
coef_one = 1.5
coef_two = -3.0 / 20.0
coef_three = 1.0 / 90.0
decay = -5.0 / 9.0
weight = 15.0 / 16.0

STATIONS, NY, WIDTH, PARTS = 32, 64, 128, 8
CUTS = 4
LENGTH = WIDTH * PARTS
ROWS = STATIONS * NY // PARTS
MIB = 1024 * 1024
SLABS = 4
LARGE = 62.75
F32, BF16 = jnp.float32, jnp.bfloat16
PAYLOAD = NY + 16

SPAN_ORDER = (5, 4, 6, 7, 0, 1, 2, 3)
ORDERS = ((3, 2, 1, 0), (2, 3, 0, 1), (2, 3, 0, 1))
SPAN_GROUPS = [list(SPAN_ORDER)]
GROUPS = (
    [[x * 16 + h * 4 + l for l in ORDERS[0]] for x in range(4) for h in range(4)],
    [[x * 16 + h * 4 + l for h in ORDERS[1]] for x in range(4) for l in range(4)],
    [[x * 16 + z for x in ORDERS[2]] for z in range(16)],
)


def span_tables():
    position = np.arange(LENGTH, dtype=np.int64)
    product = position[:, None] * position[None, 1 : LENGTH // 2 + 1] % LENGTH
    angle = product.astype(np.float32) * np.float32(2.0 * math.pi / LENGTH)
    table = np.concatenate([np.cos(angle), np.sin(angle)], axis=1).astype(BF16)
    wave = np.arange(1, LENGTH // 2 + 1).astype(np.float32) * np.float32(2.0 * math.pi / LENGTH)
    factor = -(wave * wave) / np.float32(LENGTH)
    twice = np.where(np.arange(1, LENGTH // 2 + 1) < LENGTH // 2, 2.0, 1.0).astype(np.float32)
    factor = np.concatenate([factor * twice] * 2)[None, :].astype(np.float32)
    return table, factor


def edge_kernel(rounded, first, last, sem):
    copies = [
        pltpu.make_async_copy(rounded.at[pl.ds(0, 3)], first, sem.at[0]),
        pltpu.make_async_copy(rounded.at[pl.ds(STATIONS - 3, 3)], last, sem.at[1]),
    ]
    for copy in copies:
        copy.start()
    for copy in copies:
        copy.wait()


def stencil_kernel(keep, take, far_velocity, far_register, eddy, low, high, *rest):
    base, (offset, velocity, register, sem) = rest[:CUTS], rest[CUTS:]
    step = STATIONS // CUTS
    cuts = [pl.ds(c * step, step) for c in range(CUTS)]
    loads = [
        [
            pltpu.make_async_copy(far.at[cuts[c]], near.at[cuts[c]], sem.at[k, c])
            for c in range(CUTS)
        ]
        for k, (far, near) in enumerate(((far_velocity, velocity), (far_register, register)))
    ]
    for c in range(CUTS):
        loads[0][c].start()
        loads[1][c].start()

    def plane(i):
        if i < 0:
            return low[i + 3].astype(F32)
        if i >= STATIONS:
            return high[i - STATIONS].astype(F32)
        return velocity[i]

    running = jnp.zeros((NY, WIDTH), F32)
    loads[0][0].wait()
    for c in range(CUTS):
        if c + 1 < CUTS:
            loads[0][c + 1].wait()
        loads[1][c].wait()
        for i in range(c * step, (c + 1) * step):
            here = velocity[i]
            total = (2.0 * coef_zero) * here
            for shift, coef in ((1, coef_one), (2, coef_two), (3, coef_three)):
                along = plane(i - shift) + plane(i + shift)
                across = pltpu.roll(here, shift, 0) + pltpu.roll(here, NY - shift, 0)
                total = total + coef * (along + across)
            part = decay * register[i] + eddy[i].astype(F32) * total
            base[c][i - c * step] = part
            running = keep[i] * running + take[i] * (here + weight * part)
    offset[...] = running


def span_kernel(lines, factor, _buffer, *rest):
    slabs, out, scaled, held, sem = rest[:SLABS], *rest[SLABS:]
    step = LENGTH // SLABS
    whole = jnp.concatenate([lines[SPAN_ORDER.index(b)] for b in range(PARTS)], axis=1)
    for n, slab in enumerate(slabs):
        part = jnp.dot(whole, slab[...], preferred_element_type=F32)
        scaled[n] = (part * factor[:, n * step : (n + 1) * step]).astype(BF16)
    wide = 256
    per = wide // WIDTH
    copies = [pltpu.make_async_copy(held.at[b], out.at[SPAN_ORDER.index(b)], sem.at[b]) for b in range(PARTS)]
    for n in range(LENGTH // wide):
        part = jnp.zeros((ROWS, wide), F32)
        for m, slab in enumerate(slabs):
            part = part + lax.dot_general(
                scaled[m], slab[n * wide : (n + 1) * wide, :], (((1,), (1,)), ((), ())), preferred_element_type=F32
            )
        part = part.astype(BF16)
        for b in range(per):
            held[n * per + b] = part[:, b * WIDTH : (b + 1) * WIDTH]
            copies[n * per + b].start()
    for copy in copies:
        copy.wait()


def store_payload(out, plane, gain):
    upper = gain.astype(BF16).astype(F32)
    tail = jnp.concatenate([upper, gain - upper], axis=0).astype(BF16)
    plane = plane.astype(BF16)
    for m in range(4):
        out[m, 0:NY] = plane
        out[m, NY:PAYLOAD] = tail


def offset_kernel(keep, take, second, eddy, base_offset, out):
    running = jnp.zeros((NY, WIDTH), F32)
    gain = jnp.ones((8, WIDTH), F32)
    for i in range(STATIONS):
        term = eddy[i].astype(F32) * second[i].astype(F32)
        running = keep[i] * running + (take[i] * weight) * term
        gain = gain * keep[i]
    store_payload(out, running + base_offset[...], gain)


def local_kernel(keep, take, velocity, eddy, second, _, *rest):
    base, register, local, (held, sem) = rest[:CUTS], rest[CUTS], rest[CUTS + 1 : 2 * CUTS + 1], rest[2 * CUTS + 1 :]
    step = STATIONS // CUTS
    cuts = [pl.ds(c * step, step) for c in range(CUTS)]
    copies = [pltpu.make_async_copy(held.at[cuts[c]], register.at[cuts[c]], sem.at[c]) for c in range(CUTS)]
    running = jnp.zeros((NY, WIDTH), F32)
    for c in range(CUTS):
        for i in range(c * step, (c + 1) * step):
            new = base[c][i - c * step] + eddy[i].astype(F32) * second[i].astype(F32)
            held[i] = new
            running = keep[i] * running + take[i] * (velocity[i] + weight * new)
            local[c][i - c * step] = running
        copies[c].start()
    for copy in copies:
        copy.wait()


def hold_kernel(plane, held):
    held[...] = plane[...]


def fold(place, received, order):
    total = jnp.zeros((NY, WIDTH), F32)
    gain = jnp.ones((8, WIDTH), F32)
    before, gain_before = total, gain
    for m in range(4):
        reached = place == m
        before = jnp.where(reached, total, before)
        gain_before = jnp.where(reached, gain, gain_before)
        slot = order.index(m)
        tail = received[slot, NY:PAYLOAD].astype(F32)
        one = tail[0:8] + tail[8:16]
        total = total * one[0:1] + received[slot, 0:NY].astype(F32)
        gain = gain * one
    return before, gain_before, total, gain


def fold_kernel(order, place, received, before, gain_before, out):
    one, two, total, gain = fold(place[0], received, order)
    before[...] = one
    gain_before[...] = two
    store_payload(out, total, gain)


def final_kernel(place, keep, received, before1, gain1, before2, gain2, inflow, *rest):
    local, out, done, sem = rest[:CUTS], rest[CUTS], rest[CUTS + 1], rest[CUTS + 2]
    step = STATIONS // CUTS
    cuts = [pl.ds(c * step, step) for c in range(CUTS)]
    stores = [pltpu.make_async_copy(done.at[cuts[c]], out.at[cuts[c]], sem.at[c]) for c in range(CUTS)]
    before, gain, _, _ = fold(place[0], received, ORDERS[2])
    value = before + gain[0:1] * inflow[...]
    value = before2[...] + gain2[0:1] * value
    running = before1[...] + gain1[0:1] * value
    for c in range(CUTS):
        for i in range(step):
            running = running * keep[c * step + i]
            done[c * step + i] = local[c][i] + running
        stores[c].start()
    for store in stores:
        store.wait()


SMEM = pl.BlockSpec(memory_space=pltpu.SMEM)
VMEM = pl.BlockSpec(memory_space=pltpu.VMEM)
ANY = pl.BlockSpec(memory_space=pl.ANY)
HBM = pl.BlockSpec(memory_space=pltpu.HBM)
CUBE = jax.ShapeDtypeStruct((STATIONS, NY, WIDTH), F32)
PLANE = jax.ShapeDtypeStruct((NY, WIDTH), F32)
GAIN = jax.ShapeDtypeStruct((8, WIDTH), F32)
PART = jax.ShapeDtypeStruct((STATIONS // CUTS, NY, WIDTH), F32)
EDGE = jax.ShapeDtypeStruct((3, NY, WIDTH), BF16)
DMA = pltpu.SemaphoreType.DMA
SLOTS = jax.ShapeDtypeStruct((4, PAYLOAD, WIDTH), BF16)


def call(kernel, name, in_specs, out_specs, out_shape, flops, bytes_accessed, scratch=(), limit=16, alias=None):
    return pl.pallas_call(
        kernel,
        name=name,
        in_specs=in_specs,
        out_specs=out_specs,
        out_shape=out_shape,
        scratch_shapes=scratch,
        input_output_aliases=alias or {},
        compiler_params=pltpu.CompilerParams(vmem_limit_bytes=int(limit * MIB)),
        cost_estimate=pl.CostEstimate(flops=flops, bytes_accessed=bytes_accessed, transcendentals=0),
    )


def body(velocity, register, eddy_viscosity, courant, inflow):
    table, factor = span_tables()
    place = lax.axis_index("gx")
    places = [jnp.reshape(p, (1,)) for p in (place % 4, place // 4 % 4, place // 16)]
    keep = courant / (1.0 + courant)
    take = 1.0 / (1.0 + courant)

    rounded = velocity.astype(BF16)
    first, last = call(edge_kernel, "edge", [HBM], (VMEM, VMEM), (EDGE, EDGE), 3_000_000_000, 200_000, (DMA((2,)),))(rounded)
    rounded = rounded.reshape(PARTS, ROWS, WIDTH)
    lines = lax.all_to_all(rounded, "gz", 0, 0, axis_index_groups=SPAN_GROUPS, tiled=True)

    count = lax.axis_size("gx")
    forward = [(i, i + 1) for i in range(count - 1)]
    backward = [(b, a) for a, b in forward]
    low = lax.ppermute(last, "gx", forward)
    high = lax.ppermute(first, "gx", backward)
    lines, low, high, places[0] = lax.optimization_barrier((lines, low, high, places[0]))
    *base, base_offset = call(
        stencil_kernel,
        "stencil",
        [SMEM, SMEM, HBM, HBM] + [VMEM] * 3,
        (VMEM,) * (CUTS + 1),
        (PART,) * CUTS + (PLANE,),
        8_000_000,
        4_000_000,
        (pltpu.VMEM(CUBE.shape, F32), pltpu.VMEM(CUBE.shape, F32), DMA((2, CUTS))),
        LARGE,
    )(keep, take, velocity, register, eddy_viscosity, low, high)

    base_offset = call(hold_kernel, "hold", [VMEM], VMEM, PLANE, 1000, 100_000)(base_offset)

    step = LENGTH // SLABS
    slabs = [jnp.asarray(table[:, n * step : (n + 1) * step]) for n in range(SLABS)]
    derived = call(
        span_kernel,
        "span",
        [VMEM, VMEM, HBM] + [VMEM] * SLABS,
        HBM,
        jax.ShapeDtypeStruct((PARTS, ROWS, WIDTH), BF16),
        4 * ROWS * LENGTH * LENGTH,
        3_200_000,
        (
            pltpu.VMEM((SLABS, ROWS, step), BF16),
            pltpu.VMEM((PARTS, ROWS, WIDTH), BF16),
            DMA((PARTS,)),
        ),
        alias={2: 0},
    )(lines, jnp.asarray(factor), rounded, *slabs)
    second = lax.all_to_all(derived, "gz", 0, 0, axis_index_groups=SPAN_GROUPS, tiled=True).reshape(STATIONS, NY, WIDTH)

    payload = call(offset_kernel, "offset", [SMEM, SMEM] + [VMEM] * 3, VMEM, SLOTS, 1_500_000, 1_100_000)(
        keep, take, second, eddy_viscosity, base_offset
    )
    new_register, *local = call(
        local_kernel,
        "local",
        [SMEM, SMEM] + [VMEM] * 3 + [ANY] + [VMEM] * CUTS,
        (HBM,) + (VMEM,) * CUTS,
        (CUBE,) + (PART,) * CUTS,
        3_000_000,
        5_000_000,
        (pltpu.VMEM(CUBE.shape, F32), DMA((CUTS,))),
        alias={6 + c: 1 + c for c in range(CUTS)},
    )(keep, take, velocity, eddy_viscosity, second, payload, *base)

    found = []
    for level in range(3):
        payload = lax.all_to_all(payload, "gx", 0, 0, axis_index_groups=GROUPS[level], tiled=True)
        if level < 2:
            before, gain, payload = call(
                functools.partial(fold_kernel, ORDERS[level]), "fold", [SMEM, VMEM], (VMEM,) * 3, (PLANE, GAIN, SLOTS), 200_000, 300_000
            )(places[level], payload)
            found += [before, gain]

    new_velocity = call(
        final_kernel,
        "final",
        [SMEM, SMEM] + [VMEM] * (6 + CUTS),
        HBM,
        CUBE,
        800_000,
        2_300_000,
        (pltpu.VMEM(CUBE.shape, F32), DMA((CUTS,))),
    )(places[2], keep, payload, *found, inflow, *local)
    return new_velocity, new_register


def solution(mesh):
    return jax.shard_map(
        body,
        mesh=mesh,
        in_specs=(
            P("gx", None, "gz"),
            P("gx", None, "gz"),
            P("gx", None, "gz"),
            P("gx"),
            P(None, "gz"),
        ),
        out_specs=(P("gx", None, "gz"), P("gx", None, "gz")),
        check_vma=False,
    )
```

```python
import functools
import math

import jax
import jax.numpy as jnp
import numpy as np
from jax import lax
from jax.experimental import pallas as pl
from jax.experimental.pallas import tpu as pltpu
from jax.sharding import PartitionSpec as P

coef_zero = -49.0 / 18.0
coef_one = 1.5
coef_two = -3.0 / 20.0
coef_three = 1.0 / 90.0
decay = -5.0 / 9.0
weight = 15.0 / 16.0

STATIONS, NY, WIDTH, PARTS = 32, 64, 128, 8
CUTS = 4
LENGTH = WIDTH * PARTS
ROWS = STATIONS * NY // PARTS
MIB = 1024 * 1024
SLABS = 4
LARGE = 62.75
F32, BF16 = jnp.float32, jnp.bfloat16
PAYLOAD = NY + 16

SPAN_ORDER = (5, 4, 6, 7, 0, 1, 2, 3)
ORDERS = ((3, 2, 1, 0), (2, 3, 0, 1), (2, 3, 0, 1))
SPAN_GROUPS = [list(SPAN_ORDER)]
GROUPS = (
    [[x * 16 + h * 4 + l for l in ORDERS[0]] for x in range(4) for h in range(4)],
    [[x * 16 + h * 4 + l for h in ORDERS[1]] for x in range(4) for l in range(4)],
    [[x * 16 + z for x in ORDERS[2]] for z in range(16)],
)


def span_tables():
    position = np.arange(LENGTH, dtype=np.int64)
    product = position[:, None] * position[None, 1 : LENGTH // 2 + 1] % LENGTH
    angle = product.astype(np.float32) * np.float32(2.0 * math.pi / LENGTH)
    table = np.concatenate([np.cos(angle), np.sin(angle)], axis=1).astype(BF16)
    wave = np.arange(1, LENGTH // 2 + 1).astype(np.float32) * np.float32(2.0 * math.pi / LENGTH)
    factor = -(wave * wave) / np.float32(LENGTH)
    twice = np.where(np.arange(1, LENGTH // 2 + 1) < LENGTH // 2, 2.0, 1.0).astype(np.float32)
    factor = np.concatenate([factor * twice] * 2)[None, :].astype(np.float32)
    return table, factor


def edge_kernel(rounded, first, last, sem):
    copies = [
        pltpu.make_async_copy(rounded.at[pl.ds(0, 3)], first, sem.at[0]),
        pltpu.make_async_copy(rounded.at[pl.ds(STATIONS - 3, 3)], last, sem.at[1]),
    ]
    for copy in copies:
        copy.start()
    for copy in copies:
        copy.wait()


def stencil_kernel(keep, take, far_velocity, far_register, eddy, low, high, *rest):
    base, (offset, velocity, register, sem) = rest[:CUTS], rest[CUTS:]
    step = STATIONS // CUTS
    cuts = [pl.ds(c * step, step) for c in range(CUTS)]
    loads = [
        [
            pltpu.make_async_copy(far.at[cuts[c]], near.at[cuts[c]], sem.at[k, c])
            for c in range(CUTS)
        ]
        for k, (far, near) in enumerate(((far_velocity, velocity), (far_register, register)))
    ]
    for c in range(CUTS):
        loads[0][c].start()
        loads[1][c].start()

    def plane(i):
        if i < 0:
            return low[i + 3].astype(F32)
        if i >= STATIONS:
            return high[i - STATIONS].astype(F32)
        return velocity[i]

    running = jnp.zeros((NY, WIDTH), F32)
    loads[0][0].wait()
    for c in range(CUTS):
        if c + 1 < CUTS:
            loads[0][c + 1].wait()
        loads[1][c].wait()
        for i in range(c * step, (c + 1) * step):
            here = velocity[i]
            total = (2.0 * coef_zero) * here
            for shift, coef in ((1, coef_one), (2, coef_two), (3, coef_three)):
                along = plane(i - shift) + plane(i + shift)
                across = pltpu.roll(here, shift, 0) + pltpu.roll(here, NY - shift, 0)
                total = total + coef * (along + across)
            part = decay * register[i] + eddy[i].astype(F32) * total
            base[c][i - c * step] = part
            running = keep[i] * running + take[i] * (here + weight * part)
    offset[...] = running


def span_kernel(lines, factor, _buffer, *rest):
    slabs, out, scaled, held, sem = rest[:SLABS], *rest[SLABS:]
    step = LENGTH // SLABS
    whole = jnp.concatenate([lines[SPAN_ORDER.index(b)] for b in range(PARTS)], axis=1)
    for n, slab in enumerate(slabs):
        part = jnp.dot(whole, slab[...], preferred_element_type=F32)
        scaled[n] = (part * factor[:, n * step : (n + 1) * step]).astype(BF16)
    wide = 256
    per = wide // WIDTH
    copies = [pltpu.make_async_copy(held.at[b], out.at[SPAN_ORDER.index(b)], sem.at[b]) for b in range(PARTS)]
    for n in range(LENGTH // wide):
        part = jnp.zeros((ROWS, wide), F32)
        for m, slab in enumerate(slabs):
            part = part + lax.dot_general(
                scaled[m], slab[n * wide : (n + 1) * wide, :], (((1,), (1,)), ((), ())), preferred_element_type=F32
            )
        part = part.astype(BF16)
        for b in range(per):
            held[n * per + b] = part[:, b * WIDTH : (b + 1) * WIDTH]
            copies[n * per + b].start()
    for copy in copies:
        copy.wait()


def store_payload(out, plane, gain):
    upper = gain.astype(BF16).astype(F32)
    tail = jnp.concatenate([upper, gain - upper], axis=0).astype(BF16)
    plane = plane.astype(BF16)
    for m in range(4):
        out[m, 0:NY] = plane
        out[m, NY:PAYLOAD] = tail


def offset_kernel(keep, take, second, eddy, base_offset, out):
    running = jnp.zeros((NY, WIDTH), F32)
    gain = jnp.ones((8, WIDTH), F32)
    for i in range(STATIONS):
        term = eddy[i].astype(F32) * second[i].astype(F32)
        running = keep[i] * running + (take[i] * weight) * term
        gain = gain * keep[i]
    store_payload(out, running + base_offset[...], gain)


def local_kernel(keep, take, velocity, eddy, second, _, *rest):
    base, register, local, (held, sem) = rest[:CUTS], rest[CUTS], rest[CUTS + 1 : 2 * CUTS + 1], rest[2 * CUTS + 1 :]
    step = STATIONS // CUTS
    cuts = [pl.ds(c * step, step) for c in range(CUTS)]
    copies = [pltpu.make_async_copy(held.at[cuts[c]], register.at[cuts[c]], sem.at[c]) for c in range(CUTS)]
    running = jnp.zeros((NY, WIDTH), F32)
    for c in range(CUTS):
        for i in range(c * step, (c + 1) * step):
            new = base[c][i - c * step] + eddy[i].astype(F32) * second[i].astype(F32)
            held[i] = new
            running = keep[i] * running + take[i] * (velocity[i] + weight * new)
            local[c][i - c * step] = running
        copies[c].start()
    for copy in copies:
        copy.wait()


def hold_kernel(plane, held):
    held[...] = plane[...]


def fold(place, received, order):
    total = jnp.zeros((NY, WIDTH), F32)
    gain = jnp.ones((8, WIDTH), F32)
    before, gain_before = total, gain
    for m in range(4):
        reached = place == m
        before = jnp.where(reached, total, before)
        gain_before = jnp.where(reached, gain, gain_before)
        slot = order.index(m)
        tail = received[slot, NY:PAYLOAD].astype(F32)
        one = tail[0:8] + tail[8:16]
        total = total * one[0:1] + received[slot, 0:NY].astype(F32)
        gain = gain * one
    return before, gain_before, total, gain


def fold_kernel(order, place, received, before, gain_before, out):
    one, two, total, gain = fold(place[0], received, order)
    before[...] = one
    gain_before[...] = two
    store_payload(out, total, gain)


def final_kernel(place, keep, received, before1, gain1, before2, gain2, inflow, *rest):
    local, out, done, sem = rest[:CUTS], rest[CUTS], rest[CUTS + 1], rest[CUTS + 2]
    step = STATIONS // CUTS
    cuts = [pl.ds(c * step, step) for c in range(CUTS)]
    stores = [pltpu.make_async_copy(done.at[cuts[c]], out.at[cuts[c]], sem.at[c]) for c in range(CUTS)]
    before, gain, _, _ = fold(place[0], received, ORDERS[2])
    value = before + gain[0:1] * inflow[...]
    value = before2[...] + gain2[0:1] * value
    running = before1[...] + gain1[0:1] * value
    for c in range(CUTS):
        for i in range(step):
            running = running * keep[c * step + i]
            done[c * step + i] = local[c][i] + running
        stores[c].start()
    for store in stores:
        store.wait()


SMEM = pl.BlockSpec(memory_space=pltpu.SMEM)
VMEM = pl.BlockSpec(memory_space=pltpu.VMEM)
ANY = pl.BlockSpec(memory_space=pl.ANY)
HBM = pl.BlockSpec(memory_space=pltpu.HBM)
CUBE = jax.ShapeDtypeStruct((STATIONS, NY, WIDTH), F32)
PLANE = jax.ShapeDtypeStruct((NY, WIDTH), F32)
GAIN = jax.ShapeDtypeStruct((8, WIDTH), F32)
PART = jax.ShapeDtypeStruct((STATIONS // CUTS, NY, WIDTH), F32)
EDGE = jax.ShapeDtypeStruct((3, NY, WIDTH), BF16)
DMA = pltpu.SemaphoreType.DMA
SLOTS = jax.ShapeDtypeStruct((4, PAYLOAD, WIDTH), BF16)


def call(kernel, name, in_specs, out_specs, out_shape, flops, bytes_accessed, scratch=(), limit=16, alias=None):
    return pl.pallas_call(
        kernel,
        name=name,
        in_specs=in_specs,
        out_specs=out_specs,
        out_shape=out_shape,
        scratch_shapes=scratch,
        input_output_aliases=alias or {},
        compiler_params=pltpu.CompilerParams(vmem_limit_bytes=int(limit * MIB)),
        cost_estimate=pl.CostEstimate(flops=flops, bytes_accessed=bytes_accessed, transcendentals=0),
    )


def body(velocity, register, eddy_viscosity, courant, inflow):
    table, factor = span_tables()
    place = lax.axis_index("gx")
    places = [jnp.reshape(p, (1,)) for p in (place % 4, place // 4 % 4, place // 16)]
    keep = courant / (1.0 + courant)
    take = 1.0 / (1.0 + courant)

    rounded = velocity.astype(BF16)
    first, last = call(edge_kernel, "edge", [HBM], (VMEM, VMEM), (EDGE, EDGE), 3_000_000_000, 200_000, (DMA((2,)),))(rounded)
    rounded = rounded.reshape(PARTS, ROWS, WIDTH)
    lines = lax.all_to_all(rounded, "gz", 0, 0, axis_index_groups=SPAN_GROUPS, tiled=True)

    count = lax.axis_size("gx")
    forward = [(i, i + 1) for i in range(count - 1)]
    backward = [(b, a) for a, b in forward]
    low = lax.ppermute(last, "gx", forward)
    high = lax.ppermute(first, "gx", backward)
    lines, low, high, places[0], places[1] = lax.optimization_barrier(
        (lines, low, high, places[0], places[1])
    )
    *base, base_offset = call(
        stencil_kernel,
        "stencil",
        [SMEM, SMEM, HBM, HBM] + [VMEM] * 3,
        (VMEM,) * (CUTS + 1),
        (PART,) * CUTS + (PLANE,),
        8_000_000,
        4_000_000,
        (pltpu.VMEM(CUBE.shape, F32), pltpu.VMEM(CUBE.shape, F32), DMA((2, CUTS))),
        LARGE,
    )(keep, take, velocity, register, eddy_viscosity, low, high)

    base_offset = call(hold_kernel, "hold", [VMEM], VMEM, PLANE, 1000, 100_000)(base_offset)

    step = LENGTH // SLABS
    slabs = [jnp.asarray(table[:, n * step : (n + 1) * step]) for n in range(SLABS)]
    derived = call(
        span_kernel,
        "span",
        [VMEM, VMEM, HBM] + [VMEM] * SLABS,
        HBM,
        jax.ShapeDtypeStruct((PARTS, ROWS, WIDTH), BF16),
        4 * ROWS * LENGTH * LENGTH,
        3_200_000,
        (
            pltpu.VMEM((SLABS, ROWS, step), BF16),
            pltpu.VMEM((PARTS, ROWS, WIDTH), BF16),
            DMA((PARTS,)),
        ),
        alias={2: 0},
    )(lines, jnp.asarray(factor), rounded, *slabs)
    second = lax.all_to_all(derived, "gz", 0, 0, axis_index_groups=SPAN_GROUPS, tiled=True).reshape(STATIONS, NY, WIDTH)

    payload = call(offset_kernel, "offset", [SMEM, SMEM] + [VMEM] * 3, VMEM, SLOTS, 1_500_000, 1_100_000)(
        keep, take, second, eddy_viscosity, base_offset
    )
    new_register, *local = call(
        local_kernel,
        "local",
        [SMEM, SMEM] + [VMEM] * 3 + [ANY] + [VMEM] * CUTS,
        (HBM,) + (VMEM,) * CUTS,
        (CUBE,) + (PART,) * CUTS,
        3_000_000,
        5_000_000,
        (pltpu.VMEM(CUBE.shape, F32), DMA((CUTS,))),
        alias={6 + c: 1 + c for c in range(CUTS)},
    )(keep, take, velocity, eddy_viscosity, second, payload, *base)

    found = []
    for level in range(3):
        payload = lax.all_to_all(payload, "gx", 0, 0, axis_index_groups=GROUPS[level], tiled=True)
        if level < 2:
            before, gain, payload = call(
                functools.partial(fold_kernel, ORDERS[level]), "fold", [SMEM, VMEM], (VMEM,) * 3, (PLANE, GAIN, SLOTS), 200_000, 300_000
            )(places[level], payload)
            found += [before, gain]

    new_velocity = call(
        final_kernel,
        "final",
        [SMEM, SMEM] + [VMEM] * (6 + CUTS),
        HBM,
        CUBE,
        800_000,
        2_300_000,
        (pltpu.VMEM(CUBE.shape, F32), DMA((CUTS,))),
    )(places[2], keep, payload, *found, inflow, *local)
    return new_velocity, new_register


def solution(mesh):
    return jax.shard_map(
        body,
        mesh=mesh,
        in_specs=(
            P("gx", None, "gz"),
            P("gx", None, "gz"),
            P("gx", None, "gz"),
            P("gx"),
            P(None, "gz"),
        ),
        out_specs=(P("gx", None, "gz"), P("gx", None, "gz")),
        check_vma=False,
    )
```

```python
import functools
import math

import jax
import jax.numpy as jnp
import numpy as np
from jax import lax
from jax.experimental import pallas as pl
from jax.experimental.pallas import tpu as pltpu
from jax.sharding import PartitionSpec as P

coef_zero = -49.0 / 18.0
coef_one = 1.5
coef_two = -3.0 / 20.0
coef_three = 1.0 / 90.0
decay = -5.0 / 9.0
weight = 15.0 / 16.0

STATIONS, NY, WIDTH, PARTS = 32, 64, 128, 8
CUTS = 4
LENGTH = WIDTH * PARTS
ROWS = STATIONS * NY // PARTS
MIB = 1024 * 1024
SLABS = 4
LARGE = 62.75
F32, BF16 = jnp.float32, jnp.bfloat16
PAYLOAD = NY + 16

SPAN_ORDER = (5, 4, 6, 7, 0, 1, 2, 3)
ORDERS = ((3, 2, 1, 0), (2, 3, 0, 1), (3, 2, 0, 1))
SPAN_GROUPS = [list(SPAN_ORDER)]
GROUPS = (
    [[x * 16 + h * 4 + l for l in ORDERS[0]] for x in range(4) for h in range(4)],
    [[x * 16 + h * 4 + l for h in ORDERS[1]] for x in range(4) for l in range(4)],
    [[x * 16 + z for x in ORDERS[2]] for z in range(16)],
)


def span_tables():
    position = np.arange(LENGTH, dtype=np.int64)
    product = position[:, None] * position[None, 1 : LENGTH // 2 + 1] % LENGTH
    angle = product.astype(np.float32) * np.float32(2.0 * math.pi / LENGTH)
    table = np.concatenate([np.cos(angle), np.sin(angle)], axis=1).astype(BF16)
    wave = np.arange(1, LENGTH // 2 + 1).astype(np.float32) * np.float32(2.0 * math.pi / LENGTH)
    factor = -(wave * wave) / np.float32(LENGTH)
    twice = np.where(np.arange(1, LENGTH // 2 + 1) < LENGTH // 2, 2.0, 1.0).astype(np.float32)
    factor = np.concatenate([factor * twice] * 2)[None, :].astype(np.float32)
    return table, factor


def edge_kernel(rounded, first, last, sem):
    copies = [
        pltpu.make_async_copy(rounded.at[pl.ds(0, 3)], first, sem.at[0]),
        pltpu.make_async_copy(rounded.at[pl.ds(STATIONS - 3, 3)], last, sem.at[1]),
    ]
    for copy in copies:
        copy.start()
    for copy in copies:
        copy.wait()


def stencil_kernel(keep, take, far_velocity, far_register, eddy, low, high, *rest):
    base, (offset, velocity, register, sem) = rest[:CUTS], rest[CUTS:]
    step = STATIONS // CUTS
    cuts = [pl.ds(c * step, step) for c in range(CUTS)]
    loads = [
        [
            pltpu.make_async_copy(far.at[cuts[c]], near.at[cuts[c]], sem.at[k, c])
            for c in range(CUTS)
        ]
        for k, (far, near) in enumerate(((far_velocity, velocity), (far_register, register)))
    ]
    for c in range(CUTS):
        loads[0][c].start()
        loads[1][c].start()

    def plane(i):
        if i < 0:
            return low[i + 3].astype(F32)
        if i >= STATIONS:
            return high[i - STATIONS].astype(F32)
        return velocity[i]

    running = jnp.zeros((NY, WIDTH), F32)
    loads[0][0].wait()
    for c in range(CUTS):
        if c + 1 < CUTS:
            loads[0][c + 1].wait()
        loads[1][c].wait()
        for i in range(c * step, (c + 1) * step):
            here = velocity[i]
            total = (2.0 * coef_zero) * here
            for shift, coef in ((1, coef_one), (2, coef_two), (3, coef_three)):
                along = plane(i - shift) + plane(i + shift)
                across = pltpu.roll(here, shift, 0) + pltpu.roll(here, NY - shift, 0)
                total = total + coef * (along + across)
            part = decay * register[i] + eddy[i].astype(F32) * total
            base[c][i - c * step] = part
            running = keep[i] * running + take[i] * (here + weight * part)
    offset[...] = running


def span_kernel(lines, factor, _buffer, *rest):
    slabs, out, scaled, held, sem = rest[:SLABS], *rest[SLABS:]
    step = LENGTH // SLABS
    whole = jnp.concatenate([lines[SPAN_ORDER.index(b)] for b in range(PARTS)], axis=1)
    for n, slab in enumerate(slabs):
        part = jnp.dot(whole, slab[...], preferred_element_type=F32)
        scaled[n] = (part * factor[:, n * step : (n + 1) * step]).astype(BF16)
    wide = 256
    per = wide // WIDTH
    copies = [pltpu.make_async_copy(held.at[b], out.at[SPAN_ORDER.index(b)], sem.at[b]) for b in range(PARTS)]
    for n in range(LENGTH // wide):
        part = jnp.zeros((ROWS, wide), F32)
        for m, slab in enumerate(slabs):
            part = part + lax.dot_general(
                scaled[m], slab[n * wide : (n + 1) * wide, :], (((1,), (1,)), ((), ())), preferred_element_type=F32
            )
        part = part.astype(BF16)
        for b in range(per):
            held[n * per + b] = part[:, b * WIDTH : (b + 1) * WIDTH]
            copies[n * per + b].start()
    for copy in copies:
        copy.wait()


def store_payload(out, plane, gain):
    upper = gain.astype(BF16).astype(F32)
    tail = jnp.concatenate([upper, gain - upper], axis=0).astype(BF16)
    plane = plane.astype(BF16)
    for m in range(4):
        out[m, 0:NY] = plane
        out[m, NY:PAYLOAD] = tail


def offset_kernel(keep, take, second, eddy, base_offset, out):
    running = jnp.zeros((NY, WIDTH), F32)
    gain = jnp.ones((8, WIDTH), F32)
    for i in range(STATIONS):
        term = eddy[i].astype(F32) * second[i].astype(F32)
        running = keep[i] * running + (take[i] * weight) * term
        gain = gain * keep[i]
    store_payload(out, running + base_offset[...], gain)


def local_kernel(keep, take, velocity, eddy, second, _, *rest):
    base, register, local, (held, sem) = rest[:CUTS], rest[CUTS], rest[CUTS + 1 : 2 * CUTS + 1], rest[2 * CUTS + 1 :]
    step = STATIONS // CUTS
    cuts = [pl.ds(c * step, step) for c in range(CUTS)]
    copies = [pltpu.make_async_copy(held.at[cuts[c]], register.at[cuts[c]], sem.at[c]) for c in range(CUTS)]
    running = jnp.zeros((NY, WIDTH), F32)
    for c in range(CUTS):
        for i in range(c * step, (c + 1) * step):
            new = base[c][i - c * step] + eddy[i].astype(F32) * second[i].astype(F32)
            held[i] = new
            running = keep[i] * running + take[i] * (velocity[i] + weight * new)
            local[c][i - c * step] = running
        copies[c].start()
    for copy in copies:
        copy.wait()


def hold_kernel(plane, held):
    held[...] = plane[...]


def fold(place, received, order):
    total = jnp.zeros((NY, WIDTH), F32)
    gain = jnp.ones((8, WIDTH), F32)
    before, gain_before = total, gain
    for m in range(4):
        reached = place == m
        before = jnp.where(reached, total, before)
        gain_before = jnp.where(reached, gain, gain_before)
        slot = order.index(m)
        tail = received[slot, NY:PAYLOAD].astype(F32)
        one = tail[0:8] + tail[8:16]
        total = total * one[0:1] + received[slot, 0:NY].astype(F32)
        gain = gain * one
    return before, gain_before, total, gain


def fold_kernel(order, place, received, before, gain_before, out):
    one, two, total, gain = fold(place[0], received, order)
    before[...] = one
    gain_before[...] = two
    store_payload(out, total, gain)


def final_kernel(place, keep, received, before1, gain1, before2, gain2, inflow, *rest):
    local, out, done, sem = rest[:CUTS], rest[CUTS], rest[CUTS + 1], rest[CUTS + 2]
    step = STATIONS // CUTS
    cuts = [pl.ds(c * step, step) for c in range(CUTS)]
    stores = [pltpu.make_async_copy(done.at[cuts[c]], out.at[cuts[c]], sem.at[c]) for c in range(CUTS)]
    before, gain, _, _ = fold(place[0], received, ORDERS[2])
    value = before + gain[0:1] * inflow[...]
    value = before2[...] + gain2[0:1] * value
    running = before1[...] + gain1[0:1] * value
    for c in range(CUTS):
        for i in range(step):
            running = running * keep[c * step + i]
            done[c * step + i] = local[c][i] + running
        stores[c].start()
    for store in stores:
        store.wait()


SMEM = pl.BlockSpec(memory_space=pltpu.SMEM)
VMEM = pl.BlockSpec(memory_space=pltpu.VMEM)
ANY = pl.BlockSpec(memory_space=pl.ANY)
HBM = pl.BlockSpec(memory_space=pltpu.HBM)
CUBE = jax.ShapeDtypeStruct((STATIONS, NY, WIDTH), F32)
PLANE = jax.ShapeDtypeStruct((NY, WIDTH), F32)
GAIN = jax.ShapeDtypeStruct((8, WIDTH), F32)
PART = jax.ShapeDtypeStruct((STATIONS // CUTS, NY, WIDTH), F32)
EDGE = jax.ShapeDtypeStruct((3, NY, WIDTH), BF16)
DMA = pltpu.SemaphoreType.DMA
SLOTS = jax.ShapeDtypeStruct((4, PAYLOAD, WIDTH), BF16)


def call(kernel, name, in_specs, out_specs, out_shape, flops, bytes_accessed, scratch=(), limit=16, alias=None):
    return pl.pallas_call(
        kernel,
        name=name,
        in_specs=in_specs,
        out_specs=out_specs,
        out_shape=out_shape,
        scratch_shapes=scratch,
        input_output_aliases=alias or {},
        compiler_params=pltpu.CompilerParams(vmem_limit_bytes=int(limit * MIB)),
        cost_estimate=pl.CostEstimate(flops=flops, bytes_accessed=bytes_accessed, transcendentals=0),
    )


def body(velocity, register, eddy_viscosity, courant, inflow):
    table, factor = span_tables()
    place = lax.axis_index("gx")
    places = [jnp.reshape(p, (1,)) for p in (place % 4, place // 4 % 4, place // 16)]
    keep = courant / (1.0 + courant)
    take = 1.0 / (1.0 + courant)

    rounded = velocity.astype(BF16)
    first, last = call(edge_kernel, "edge", [HBM], (VMEM, VMEM), (EDGE, EDGE), 3_000_000_000, 200_000, (DMA((2,)),))(rounded)
    rounded = rounded.reshape(PARTS, ROWS, WIDTH)
    lines = lax.all_to_all(rounded, "gz", 0, 0, axis_index_groups=SPAN_GROUPS, tiled=True)

    count = lax.axis_size("gx")
    forward = [(i, i + 1) for i in range(count - 1)]
    backward = [(b, a) for a, b in forward]
    low = lax.ppermute(last, "gx", forward)
    high = lax.ppermute(first, "gx", backward)
    lines, low, high, places[0], places[1] = lax.optimization_barrier(
        (lines, low, high, places[0], places[1])
    )
    *base, base_offset = call(
        stencil_kernel,
        "stencil",
        [SMEM, SMEM, HBM, HBM] + [VMEM] * 3,
        (VMEM,) * (CUTS + 1),
        (PART,) * CUTS + (PLANE,),
        8_000_000,
        4_000_000,
        (pltpu.VMEM(CUBE.shape, F32), pltpu.VMEM(CUBE.shape, F32), DMA((2, CUTS))),
        LARGE,
    )(keep, take, velocity, register, eddy_viscosity, low, high)

    base_offset = call(hold_kernel, "hold", [VMEM], VMEM, PLANE, 1000, 100_000)(base_offset)

    step = LENGTH // SLABS
    slabs = [jnp.asarray(table[:, n * step : (n + 1) * step]) for n in range(SLABS)]
    derived = call(
        span_kernel,
        "span",
        [VMEM, VMEM, HBM] + [VMEM] * SLABS,
        HBM,
        jax.ShapeDtypeStruct((PARTS, ROWS, WIDTH), BF16),
        4 * ROWS * LENGTH * LENGTH,
        3_200_000,
        (
            pltpu.VMEM((SLABS, ROWS, step), BF16),
            pltpu.VMEM((PARTS, ROWS, WIDTH), BF16),
            DMA((PARTS,)),
        ),
        alias={2: 0},
    )(lines, jnp.asarray(factor), rounded, *slabs)
    second = lax.all_to_all(derived, "gz", 0, 0, axis_index_groups=SPAN_GROUPS, tiled=True).reshape(STATIONS, NY, WIDTH)

    payload = call(offset_kernel, "offset", [SMEM, SMEM] + [VMEM] * 3, VMEM, SLOTS, 1_500_000, 1_100_000)(
        keep, take, second, eddy_viscosity, base_offset
    )
    new_register, *local = call(
        local_kernel,
        "local",
        [SMEM, SMEM] + [VMEM] * 3 + [ANY] + [VMEM] * CUTS,
        (HBM,) + (VMEM,) * CUTS,
        (CUBE,) + (PART,) * CUTS,
        3_000_000,
        5_000_000,
        (pltpu.VMEM(CUBE.shape, F32), DMA((CUTS,))),
        alias={6 + c: 1 + c for c in range(CUTS)},
    )(keep, take, velocity, eddy_viscosity, second, payload, *base)

    found = []
    for level in range(3):
        payload = lax.all_to_all(payload, "gx", 0, 0, axis_index_groups=GROUPS[level], tiled=True)
        if level < 2:
            before, gain, payload = call(
                functools.partial(fold_kernel, ORDERS[level]), "fold", [SMEM, VMEM], (VMEM,) * 3, (PLANE, GAIN, SLOTS), 200_000, 300_000
            )(places[level], payload)
            found += [before, gain]

    new_velocity = call(
        final_kernel,
        "final",
        [SMEM, SMEM] + [VMEM] * (6 + CUTS),
        HBM,
        CUBE,
        800_000,
        2_300_000,
        (pltpu.VMEM(CUBE.shape, F32), DMA((CUTS,))),
    )(places[2], keep, payload, *found, inflow, *local)
    return new_velocity, new_register


def solution(mesh):
    return jax.shard_map(
        body,
        mesh=mesh,
        in_specs=(
            P("gx", None, "gz"),
            P("gx", None, "gz"),
            P("gx", None, "gz"),
            P("gx"),
            P(None, "gz"),
        ),
        out_specs=(P("gx", None, "gz"), P("gx", None, "gz")),
        check_vma=False,
    )
```
